512 devices in a mesh: seq: 64 (over z, x_hi, core), tp: 4 (over y), pair: 2 (over x_lo).
Axes of the slice: x: 4 (x_hi: 2, x_lo: 2; x = x_hi * 2 + x_lo), y: 4, z: 16, core: 2. Of those that a mesh axis runs over, the one named last changes fastest.
Arguments:
- queries: bfloat16 [8192, 4096], P('seq', ('tp', 'pair')), may hold values from -18 to 18
- stored_key_value: bfloat16 [8192, 1024], P('seq', ('tp', 'pair')), may hold values from -18 to 18, as said below
- out_grad: bfloat16 [8192, 4096], P('seq', ('tp', 'pair')), may hold values from -6 to 6
- attn_out: bfloat16 [8192, 4096], P('seq', ('tp', 'pair')), may hold values from -3 to 3
- segment_ids: int32 [8192], P('seq'), may hold values from 0 to 5, as said below
- loss_mask: int32 [8192], P('seq'), may hold values 0 or 1
Outputs:
- query_gradient: bfloat16 [8192, 4096], P('seq', ('tp', 'pair'))
- kv_grad: bfloat16 [8192, 1024], P('seq', ('tp', 'pair'))
The draws below stay inside these ranges and needn't reach their ends.
Inputs may be any that keep to these rules, and one draw needn't show every extreme that they name: `stored_key_value`: each row of a key-value head's keys lies within the range. `segment_ids`: document numbers never decrease along the row; each document is contiguous; the first document holds exactly 6144 tokens and the others share the rest, each of one token or more.
All inputs are finite; a program needn't handle non-finite values. No bound on the sum of `loss_mask` on one device may be relied on, other than what follows from the above.
Results may differ from the reference program's by a relative error of at most 0.007.
Values may be sent and summed in bfloat16 or wider, within the bound.
No kernel may reach another device: no remote copies, remote signals or barrier semaphores. Data moves between devices by JAX's collectives and lax.ppermute only.
A program may use at most 64 MiB of HBM per device.

```python
import math
import jax
import jax.numpy as jnp
from jax import lax

HEAD_WIDTH = 128
QUERY_HEADS = 32
KEY_VALUE_HEADS = 4
DOCS = 6
TOK_DEV = 128
ROW_LENGTH = 8192


def shared_base(key):
    random_jitter = jax.random.normal(key, (ROW_LENGTH, KEY_VALUE_HEADS, HEAD_WIDTH), jnp.float32)
    return jnp.clip(random_jitter, -3.0, 3.0)


def sink_direction(base):
    return jnp.where(base[0] >= 0.0, 1.0, -1.0)


def draw_stored_key_value(key, part):
    base = shared_base(key)
    direction = sink_direction(base)
    key = jax.random.fold_in(key, 11)
    first_key_half, second_key_half = jax.random.split(key)
    positions = jnp.arange(ROW_LENGTH, dtype=jnp.int32)
    sink_rows = positions < TOK_DEV
    unscaled_keys = jnp.clip(jax.random.normal(first_key_half, (ROW_LENGTH, KEY_VALUE_HEADS, HEAD_WIDTH), jnp.float32), -4.0, 4.0)
    sink_keys = direction[None] + 0.7 * unscaled_keys
    unscaled_keys = jnp.where(sink_rows[:, None, None], sink_keys, unscaled_keys)
    value_rows = jnp.clip(jax.random.normal(second_key_half, (ROW_LENGTH, KEY_VALUE_HEADS, HEAD_WIDTH), jnp.float32), -4.0, 4.0)
    stacked_grads = jnp.stack([unscaled_keys, value_rows], axis=2)
    return stacked_grads.reshape(ROW_LENGTH, KEY_VALUE_HEADS * 2 * HEAD_WIDTH).astype(jnp.bfloat16)


def draw_queries(key, part):
    base = shared_base(key)
    direction = sink_direction(base)
    key = jax.random.fold_in(key, 23)
    group_width = QUERY_HEADS // KEY_VALUE_HEADS
    lift = math.log(0.5 * ROW_LENGTH / TOK_DEV + 1.0) / math.sqrt(HEAD_WIDTH)
    lifted = lift * jnp.repeat(direction, group_width, axis=0)[None]
    drawn = jnp.clip(jax.random.normal(key, (ROW_LENGTH, QUERY_HEADS, HEAD_WIDTH), jnp.float32), -4.0, 4.0) + lifted
    return drawn.reshape(ROW_LENGTH, QUERY_HEADS * HEAD_WIDTH).astype(jnp.bfloat16)


def draw_segment_ids(key, part):
    key = jax.random.fold_in(key, 37)
    first_length = 3 * ROW_LENGTH // 4
    rest_length = ROW_LENGTH - first_length
    shuffled = jax.random.permutation(key, rest_length - 1).astype(jnp.int32)
    cut_points = jnp.sort(shuffled[:DOCS - 2] + 1)
    starts = jnp.concatenate([jnp.zeros((1,), jnp.int32), cut_points]) + first_length
    positions = jnp.arange(ROW_LENGTH, dtype=jnp.int32)
    return jnp.sum((positions[:, None] >= starts[None, :]).astype(jnp.int32), axis=1).astype(jnp.int32)


def set_ends(drawn, key, smallest, top_value):
    longest = drawn.shape.index(max(drawn.shape))
    spots = []
    for shift in (0, 1):
        where = [jax.random.randint(jax.random.fold_in(key, axis), (), 0, length) for axis, length in enumerate(drawn.shape)]
        where[longest] = (where[longest] + shift) % drawn.shape[longest]
        spots.append(tuple(where))
    return drawn.at[spots[0]].set(smallest).at[spots[1]].set(top_value)


def shard_levels(own_key, shape, cuts, low, high):
    def one(axis_at, shards_of):
        draws = jax.random.uniform(jax.random.fold_in(jax.random.fold_in(own_key, 6), axis_at), (shards_of,), jnp.float32, low / len(cuts), high / len(cuts))
        return jnp.repeat(jnp.exp(draws), shape[axis_at] // shards_of).reshape((-1,) + (1,) * (len(shape) - axis_at - 1))

    level = one(*cuts[0])
    for cut in cuts[1:]:
        level = level * one(*cut)
    return level


def centred(stream_key, extent, spread, most, pieces=(), held_as=jnp.bfloat16):
    level = shard_levels(stream_key, extent, pieces, -0.22, 0.18) if pieces else 1.0
    entries = jax.random.normal(stream_key, extent, jnp.float32) * spread * level
    return jnp.minimum(jnp.maximum(entries, -most), most).astype(held_as)


def setup_inputs(seed: int = 0) -> dict:
    streams_of = jax.random.split(jax.random.key(seed), 7)
    return {
        "queries": draw_queries(jax.random.fold_in(streams_of[6], 71), 0),
        "stored_key_value": draw_stored_key_value(jax.random.fold_in(streams_of[6], 71), 0),
        "out_grad": centred(streams_of[2], (ROW_LENGTH, QUERY_HEADS * HEAD_WIDTH), 1.0, 6.0, ((0, 64), (1, 8))),
        "attn_out": centred(streams_of[3], (ROW_LENGTH, QUERY_HEADS * HEAD_WIDTH), 0.5, 3.0, ((0, 64), (1, 8))),
        "segment_ids": draw_segment_ids(jax.random.fold_in(streams_of[6], 71), 0),
        "loss_mask": set_ends((jax.random.randint(streams_of[5], (ROW_LENGTH,), 0, 4) < 3).astype(jnp.int32), jax.random.fold_in(streams_of[5], 1), 0, 1),
    }


NEGATIVE = -1e+30

def head_terms(q_one, k_one, v_one, cot_one, delta_one, allowed, scale_factor):
    scores = jnp.dot(q_one, k_one.T, preferred_element_type=jnp.float32) * scale_factor
    scores = jnp.where(allowed, scores, NEGATIVE)
    row_max = lax.optimization_barrier(jnp.max(scores, axis=1, keepdims=True))
    total = lax.optimization_barrier(jnp.sum(jnp.where(allowed, jnp.exp(scores - row_max), 0.0), axis=1, keepdims=True))
    log_norm = row_max + jnp.log(total)
    softmax_w = jnp.where(allowed, jnp.exp(scores - log_norm), 0.0)
    grad_probs = jnp.dot(cot_one, v_one.T, preferred_element_type=jnp.float32)
    grad_scores = (scale_factor * softmax_w * (grad_probs - delta_one[:, None])).astype(jnp.bfloat16)
    grad_q = jnp.dot(grad_scores, k_one, preferred_element_type=jnp.float32)
    return (grad_q, grad_scores, softmax_w.astype(jnp.bfloat16))

def rounded(value_rows):
    return lax.optimization_barrier(value_rows.astype(jnp.bfloat16)).astype(jnp.float32)

def reference(queries, stored_key_value, out_grad, attn_out, segment_ids, loss_mask):
    group_width = QUERY_HEADS // KEY_VALUE_HEADS
    half_size = group_width // 2
    half_count = QUERY_HEADS // half_size
    scale_factor = 1.0 / math.sqrt(HEAD_WIDTH)
    q_all = jnp.transpose(queries.reshape(ROW_LENGTH, QUERY_HEADS, HEAD_WIDTH), (1, 0, 2))
    key_value_rows = stored_key_value.reshape(ROW_LENGTH, KEY_VALUE_HEADS, 2, HEAD_WIDTH)
    k_all = jnp.transpose(key_value_rows[:, :, 0, :], (1, 0, 2))
    v_all = jnp.transpose(key_value_rows[:, :, 1, :], (1, 0, 2))
    cotangent = out_grad * loss_mask[:, None].astype(jnp.bfloat16)
    cot_all = jnp.transpose(cotangent.reshape(ROW_LENGTH, QUERY_HEADS, HEAD_WIDTH), (1, 0, 2))
    out_all = jnp.transpose(attn_out.reshape(ROW_LENGTH, QUERY_HEADS, HEAD_WIDTH), (1, 0, 2))
    delta_all = lax.optimization_barrier(jnp.sum(cot_all.astype(jnp.float32) * out_all.astype(jnp.float32), axis=2))
    q_block = min(4 * TOK_DEV, ROW_LENGTH)
    sub_count = q_block // TOK_DEV
    positions = jnp.arange(ROW_LENGTH, dtype=jnp.int32)
    key_grand_sum = jnp.zeros((KEY_VALUE_HEADS, ROW_LENGTH, HEAD_WIDTH), jnp.float32)
    value_grand_sum = jnp.zeros((KEY_VALUE_HEADS, ROW_LENGTH, HEAD_WIDTH), jnp.float32)
    query_parts = []
    for blk_index in range(ROW_LENGTH // q_block):
        row_low = blk_index * q_block
        row_upper = row_low + q_block
        allowed = (positions[None, :row_upper] <= positions[row_low:row_upper, None]) & (segment_ids[None, :row_upper] == segment_ids[row_low:row_upper, None])
        k_part = k_all[:, :row_upper]
        v_part = v_all[:, :row_upper]

        def per_half(operands):
            q_half, cot_half, delta_half, half_id = operands
            group_id = half_id // 2
            side = half_id % 2
            k_one = lax.dynamic_index_in_dim(k_part, group_id, 0, keepdims=False)
            v_one = lax.dynamic_index_in_dim(v_part, group_id, 0, keepdims=False)

            def per_head(carry, head_ops):
                k_acc, v_acc = carry
                q_one, cot_one, delta_one = head_ops
                grad_q, grad_scores, weights_b = head_terms(q_one, k_one, v_one, cot_one, delta_one, allowed, scale_factor)
                q_sub = q_one.reshape(sub_count, TOK_DEV, HEAD_WIDTH).astype(jnp.float32)
                cot_sub = cot_one.reshape(sub_count, TOK_DEV, HEAD_WIDTH).astype(jnp.float32)
                k_acc = k_acc + jnp.einsum('stw,std->swd', grad_scores.reshape(sub_count, TOK_DEV, row_upper).astype(jnp.float32), q_sub)
                v_acc = v_acc + jnp.einsum('stw,std->swd', weights_b.reshape(sub_count, TOK_DEV, row_upper).astype(jnp.float32), cot_sub)
                return ((k_acc, v_acc), grad_q)
            zero_fill = jnp.zeros((sub_count, row_upper, HEAD_WIDTH), jnp.float32)
            (k_acc, v_acc), grad_q = lax.scan(per_head, (zero_fill, zero_fill), (q_half, cot_half, delta_half))
            k_sum = lax.optimization_barrier(jnp.sum(jnp.where(side == 0, k_acc, rounded(k_acc)), axis=0))
            v_sum = lax.optimization_barrier(jnp.sum(jnp.where(side == 1, v_acc, rounded(v_acc)), axis=0))
            return (grad_q, k_sum, v_sum)
        q_rows = q_all[:, row_low:row_upper].reshape(half_count, half_size, q_block, HEAD_WIDTH)
        cot_rows = cot_all[:, row_low:row_upper].reshape(half_count, half_size, q_block, HEAD_WIDTH)
        delta_rows = delta_all[:, row_low:row_upper].reshape(half_count, half_size, q_block)
        grad_q, key_partial_sums, value_partial_sums = lax.map(per_half, (q_rows, cot_rows, delta_rows, jnp.arange(half_count, dtype=jnp.int32)))
        query_parts.append(grad_q.reshape(QUERY_HEADS, q_block, HEAD_WIDTH))
        key_gradient = lax.optimization_barrier(jnp.sum(key_partial_sums.reshape(KEY_VALUE_HEADS, 2, row_upper, HEAD_WIDTH), axis=1))
        value_gradient = lax.optimization_barrier(jnp.sum(value_partial_sums.reshape(KEY_VALUE_HEADS, 2, row_upper, HEAD_WIDTH), axis=1))
        key_grand_sum = key_grand_sum + jnp.pad(key_gradient, ((0, 0), (0, ROW_LENGTH - row_upper), (0, 0)))
        value_grand_sum = value_grand_sum + jnp.pad(value_gradient, ((0, 0), (0, ROW_LENGTH - row_upper), (0, 0)))
    query_gradient = jnp.transpose(jnp.concatenate(query_parts, axis=1), (1, 0, 2)).reshape(ROW_LENGTH, QUERY_HEADS * HEAD_WIDTH)
    key_value_sum = jnp.transpose(jnp.stack([key_grand_sum, value_grand_sum], axis=2), (1, 0, 2, 3))
    return (query_gradient.astype(jnp.bfloat16), key_value_sum.reshape(ROW_LENGTH, KEY_VALUE_HEADS * 2 * HEAD_WIDTH).astype(jnp.bfloat16))
```

```python
import functools
import math

import jax
import jax.numpy as jnp
from jax import lax
from jax.experimental import pallas as pl
from jax.experimental.pallas import tpu as pltpu
from jax.sharding import Mesh, PartitionSpec as P

BF = jnp.bfloat16
F32 = jnp.float32
NEGATIVE = -1e30
TOK = 128
HEAD = 128
HEADS = 4
COLS = HEADS * TOK
GROUP = 4
SLOTS = 3
HALF = TOK // 2
KEYS = GROUP * HALF
Q_ROWS = 2 * COLS + 16
KV_ROWS = SLOTS * HALF + 16
SCALE = 1.0 / math.sqrt(HEAD)
SCALE2 = SCALE * math.log2(math.e)
LOG_SCALE = math.log2(SCALE)
X_AXES = ("xh", "pair")
PLANE = ("xh", "core", "pair")
NT = (((1,), (1,)), ((), ()))
NN = (((1,), (0,)), ((), ()))
VMEM_LIMIT = 56 * 1024 * 1024


def dot(a, b, dims):
    return lax.dot_general(a, b, dims, preferred_element_type=F32)


def call(kernel, name, out_shape, scratch=()):
    return pl.pallas_call(
        kernel,
        out_shape=out_shape,
        scratch_shapes=scratch,
        name=name,
        compiler_params=pltpu.CompilerParams(vmem_limit_bytes=VMEM_LIMIT),
    )


def shape(dims, dtype):
    return jax.ShapeDtypeStruct(dims, dtype)


def pack_queries(q_ref, g_ref, o_ref, seg_ref, mask_ref, out_ref):
    mask = jnp.broadcast_to(mask_ref[...].astype(F32), (TOK, TOK)).T
    rows = []
    for h in range(HEADS):
        lanes = slice(h * HEAD, (h + 1) * HEAD)
        cot = g_ref[:, lanes].astype(F32) * mask
        rows.append(jnp.sum((cot * o_ref[:, lanes].astype(F32)).T, axis=0, keepdims=True))
        cot = cot.astype(BF)
        for x in range(4):
            out_ref[x, h * TOK : (h + 1) * TOK, :] = q_ref[:, lanes]
            out_ref[x, COLS + h * TOK : COLS + (h + 1) * TOK, :] = cot
    delta = jnp.concatenate(rows, axis=0)
    high = delta.astype(BF).astype(F32)
    low = delta - high
    tail = jnp.concatenate(
        [high, low, seg_ref[...].astype(F32), jnp.zeros((7, TOK), F32)], axis=0
    ).astype(BF)
    for x in range(4):
        out_ref[x, 2 * COLS :, :] = tail


def pack_keys(own_ref, one_ref, two_ref, seg_ref, out_ref):
    tail = jnp.concatenate(
        [seg_ref[...].astype(F32), jnp.zeros((15, TOK), F32)], axis=0
    ).astype(BF)
    for s, ref in enumerate((own_ref, one_ref, two_ref)):
        for half in range(2):
            part = ref[half * HALF : (half + 1) * HALF, :]
            for r in range(GROUP):
                out_ref[2 * r + half, s * HALF : (s + 1) * HALF, :] = part
    for i in range(2 * GROUP):
        out_ref[i, SLOTS * HALF :, :] = tail


def position():
    return (
        lax.axis_index("zg"),
        lax.axis_index("zr"),
        lax.axis_index("xh"),
        lax.axis_index("core"),
        lax.axis_index("pair"),
    )


def slot_count(zg):
    return jnp.where(zg == 3, 1, zg + 1)


def key_block(kv_ref, kind, s):
    first = s * HALF if isinstance(s, int) else pl.multiple_of(s * HALF, HALF)
    return kv_ref[:, kind, pl.ds(first, HALF), :].reshape(KEYS, HEAD)


def key_segments(kv_ref, pair, turn_ref, seg_ref):
    for r in range(GROUP):
        row = kv_ref[r, 0, SLOTS * HALF :, :].astype(F32)[0:1]
        turn_ref[...] = jnp.broadcast_to(row, (TOK, TOK)).T
        seg_ref[r * HALF : (r + 1) * HALF, :] = turn_ref[
            pl.ds(pl.multiple_of(pair * HALF, HALF), HALF), :
        ]


def allowed_pairs(place, q_ref, x, other, seg_ref):
    zg, zr, xh, core, pair = place
    row = lax.broadcasted_iota(jnp.int32, (KEYS, TOK), 0)
    key_pos = (row // HALF) * 512 + row % HALF + ((2 * xh + core) * TOK + pair * HALF)
    from_core = (1 - core) if other else core
    lane = lax.broadcasted_iota(jnp.int32, (KEYS, TOK), 1)
    query_pos = lane + (zr * 512 + (2 * (x // 2) + from_core) * TOK)
    query_seg = q_ref[x, 2 * COLS :, :].astype(F32)[8:9]
    return (key_pos <= query_pos) & (seg_ref[...] == query_seg)


def tiled(mask):
    return jnp.concatenate([mask] * HEADS, axis=1)


def row_sums(same_ref, other_ref, kv_ref, out_ref, turn_ref, seg_ref):
    place = position()
    zg, zr, xh, core, pair = place
    count = slot_count(zg)
    key_segments(kv_ref, pair, turn_ref, seg_ref)

    for other, q_ref in enumerate((same_ref, other_ref)):
        from_core = (1 - core) if other else core

        def source(x, _, q_ref=q_ref, other=other, from_core=from_core):
            q = q_ref[x, :COLS, :]
            allowed = tiled(allowed_pairs(place, q_ref, x, other, seg_ref))
            s = dot(key_block(kv_ref, 0, 0), q, NT) * SCALE2
            s = jnp.where(allowed, s, NEGATIVE)
            top = jnp.maximum(jnp.max(s, axis=0, keepdims=True), 0.1 * NEGATIVE)
            total = jnp.sum(jnp.exp2(s - top), axis=0, keepdims=True)

            def block(j, state):
                top, total = state
                s = dot(key_block(kv_ref, 0, j), q, NT) * SCALE2
                new_top = jnp.maximum(top, jnp.max(s, axis=0, keepdims=True))
                part = jnp.sum(jnp.exp2(s - new_top), axis=0, keepdims=True)
                return new_top, total * jnp.exp2(top - new_top) + part

            top, total = lax.fori_loop(1, count, block, (top, total))
            norm = jnp.maximum(top + jnp.log2(total), NEGATIVE)
            for h in range(HEADS):
                piece = jnp.broadcast_to(norm[:, h * TOK : (h + 1) * TOK], (8, TOK))
                out_ref[:, from_core, x, h : h + 1, :] = piece.reshape(8, 1, TOK)
            return 0

        lax.fori_loop(0, 4, source, 0)


def gradients(
    same_ref, other_ref, kv_ref, norm_ref,
    dq_same_ref, dq_other_ref, dkv_ref,
    turn_ref, seg_ref, log_ref, turned_ref, dk_ref, dv_ref,
):
    place = position()
    zg, zr, xh, core, pair = place
    count = slot_count(zg)
    key_segments(kv_ref, pair, turn_ref, seg_ref)
    norms = norm_ref[...]
    top = jnp.max(norms, axis=0)
    log_ref[...] = top + jnp.log2(jnp.sum(jnp.exp2(norms - top[None]), axis=0)) - LOG_SCALE
    for s in range(SLOTS):
        turned_ref[s] = key_block(kv_ref, 0, s).astype(F32).T.astype(BF)
    dk_ref[...] = jnp.zeros_like(dk_ref)
    dv_ref[...] = jnp.zeros_like(dv_ref)

    for other, q_ref, dq_ref in ((1, other_ref, dq_other_ref), (0, same_ref, dq_same_ref)):
        from_core = (1 - core) if other else core

        def source(x, _, q_ref=q_ref, dq_ref=dq_ref, other=other, from_core=from_core):
            q = q_ref[x, :COLS, :]
            cot = q_ref[x, COLS : 2 * COLS, :]
            tail = q_ref[x, 2 * COLS :, :].astype(F32)
            delta = tail[0:HEADS] + tail[HEADS : 2 * HEADS]
            delta = jnp.concatenate([delta[h : h + 1] for h in range(HEADS)], axis=1)
            norms = log_ref[from_core, x]
            norm = jnp.concatenate([norms[h : h + 1] for h in range(HEADS)], axis=1)

            def block(j, allowed):
                s = dot(key_block(kv_ref, 0, j), q, NT)
                prob = jnp.exp2(s * SCALE2 - norm)
                if allowed is not None:
                    prob = jnp.where(allowed, prob, 0.0)
                dprob = dot(key_block(kv_ref, 1, j), cot, NT)
                dscore = (prob * (dprob - delta)).astype(BF)
                dk_ref[j] += dot(dscore, q, NN)
                dv_ref[j] += dot(prob.astype(BF), cot, NN)
                return dot(turned_ref[j], dscore, NN)

            dq = block(0, tiled(allowed_pairs(place, q_ref, x, other, seg_ref)))
            dq = lax.fori_loop(1, count, lambda j, dq: dq + block(j, None), dq)
            dq_ref[x] = dq.astype(BF)
            return 0

        lax.fori_loop(0, 4, source, 0)

    for s in range(SLOTS):
        for r in range(GROUP):
            rows = slice(r * HALF, (r + 1) * HALF)
            dkv_ref[2 * r, s] = dk_ref[s, rows, :].astype(BF)
            dkv_ref[2 * r + 1, s] = (dv_ref[s, rows, :] * (1.0 / SCALE)).astype(BF)


def add_parts(dkv_ref, same_ref, other_ref, own_ref, one_ref, two_ref, dq_ref):
    for s, ref in enumerate((own_ref, one_ref, two_ref)):
        for half in range(2):
            total = dkv_ref[half, s].astype(F32)
            for r in range(1, GROUP):
                total += dkv_ref[2 * r + half, s].astype(F32)
            ref[half * HALF : (half + 1) * HALF, :] = total.astype(ref.dtype)
    dq_ref[...] = (same_ref[...].astype(F32) + other_ref[...].astype(F32)).astype(BF)


def finish(dq_ref, own_ref, one_ref, two_ref, out_q_ref, out_kv_ref):
    total = dq_ref[0].astype(F32)
    for x in range(1, 4):
        total += dq_ref[x].astype(F32)
    for h in range(HEADS):
        lanes = slice(h * HEAD, (h + 1) * HEAD)
        out_q_ref[:, lanes] = total[:, lanes].T.astype(BF)
    out_kv_ref[...] = (
        own_ref[...] + one_ref[...].astype(F32) + two_ref[...].astype(F32)
    ).astype(BF)


def per_device(queries, stored_key_value, out_grad, attn_out, segment_ids, loss_mask):
    seg = segment_ids.reshape(1, TOK)
    mask = loss_mask.reshape(1, TOK)
    swap = [(0, 1), (1, 0)]

    one = lax.ppermute(stored_key_value, "zg", [(0, 1), (1, 2)])
    two = lax.ppermute(stored_key_value, "zg", [(0, 2)])
    packed = call(pack_queries, "pack_queries", shape((4, Q_ROWS, HEAD), BF))(
        queries, out_grad, attn_out, seg, mask
    )
    same = lax.all_to_all(packed, X_AXES, 0, 0, tiled=True)
    other = lax.ppermute(same, "core", swap)
    kv_packed = call(pack_keys, "pack_keys", shape((2 * GROUP, KV_ROWS, HEAD), BF))(
        stored_key_value, one, two, seg
    )
    kv = lax.all_to_all(kv_packed, ("zr", "pair"), 0, 0, tiled=True)
    kv = kv.reshape(GROUP, 2, KV_ROWS, HEAD)

    segs = [pltpu.VMEM((TOK, TOK), F32), pltpu.VMEM((KEYS, TOK), F32)]
    norms = call(row_sums, "row_sums", shape((8, 2, 4, HEADS, TOK), F32), segs)(same, other, kv)
    norms = lax.all_to_all(norms, PLANE, 0, 0, tiled=True)

    dq_same, dq_other, dkv = call(
        gradients,
        "gradients",
        (
            shape((4, HEAD, COLS), BF),
            shape((4, HEAD, COLS), BF),
            shape((2 * GROUP, SLOTS, HALF, HEAD), BF),
        ),
        segs
        + [
            pltpu.VMEM((2, 4, HEADS, TOK), F32),
            pltpu.VMEM((SLOTS, HEAD, KEYS), BF),
            pltpu.VMEM((SLOTS, KEYS, HEAD), F32),
            pltpu.VMEM((SLOTS, KEYS, HEAD), F32),
        ],
    )(same, other, kv, norms)
    dq_other = lax.ppermute(dq_other, "core", swap)
    dkv = lax.all_to_all(dkv, ("zr", "pair"), 0, 0, tiled=True)

    own, one, two, dq = call(
        add_parts,
        "add_parts",
        (
            shape((TOK, HEAD), F32),
            shape((TOK, HEAD), BF),
            shape((TOK, HEAD), BF),
            shape((4, HEAD, COLS), BF),
        ),
    )(dkv, dq_same, dq_other)
    one = lax.ppermute(one, "zg", [(1, 0), (2, 1)])
    two = lax.ppermute(two, "zg", [(2, 0)])
    dq = lax.all_to_all(dq, X_AXES, 0, 0, tiled=True)
    return call(
        finish, "finish", (shape((TOK, HEADS * HEAD), BF), shape((TOK, HEAD), BF))
    )(dq, own, one, two)


def solution(mesh):
    fine = Mesh(
        mesh.devices.reshape(4, 4, 2, 2, 4, 2), ("zg", "zr", "xh", "core", "tp", "pair")
    )
    rows = ("zg", "zr", "xh", "core")
    wide = P(rows, ("tp", "pair"))
    return jax.shard_map(
        per_device,
        mesh=fine,
        in_specs=(wide, wide, wide, wide, P(rows), P(rows)),
        out_specs=(wide, wide),
        check_vma=False,
    )
```

```python
import functools
import math

import jax
import jax.numpy as jnp
from jax import lax
from jax.experimental import pallas as pl
from jax.experimental.pallas import tpu as pltpu
from jax.sharding import Mesh, PartitionSpec as P

BF = jnp.bfloat16
F32 = jnp.float32
NEGATIVE = -1e30
TOK = 128
HEAD = 128
HEADS = 4
COLS = HEADS * TOK
GROUP = 4
SLOTS = 3
HALF = TOK // 2
KEYS = GROUP * HALF
Q_ROWS = 2 * COLS + 16
KV_ROWS = SLOTS * HALF + 16
SCALE = 1.0 / math.sqrt(HEAD)
SCALE2 = SCALE * math.log2(math.e)
LOG_SCALE = math.log2(SCALE)
X_AXES = ("xh", "pair")
PLANE = ("xh", "core", "pair")
NT = (((1,), (1,)), ((), ()))
NN = (((1,), (0,)), ((), ()))
VMEM_LIMIT = 32 * 1024 * 1024


def dot(a, b, dims):
    return lax.dot_general(a, b, dims, preferred_element_type=F32)


def near(array):
    return pltpu.with_memory_space_constraint(array, pltpu.VMEM)


def call(kernel, name, out_shape, scratch=(), resident=()):
    run = pl.pallas_call(
        kernel,
        out_shape=out_shape,
        scratch_shapes=scratch,
        name=name,
        compiler_params=pltpu.CompilerParams(vmem_limit_bytes=VMEM_LIMIT),
    )
    return lambda *args: run(*(near(a) if i in resident else a for i, a in enumerate(args)))


def shape(dims, dtype):
    return jax.ShapeDtypeStruct(dims, dtype)


def pack_queries(q_ref, g_ref, o_ref, seg_ref, mask_ref, out_ref):
    mask = jnp.broadcast_to(mask_ref[...].astype(F32), (TOK, TOK)).T
    rows = []
    for h in range(HEADS):
        lanes = slice(h * HEAD, (h + 1) * HEAD)
        cot = g_ref[:, lanes].astype(F32) * mask
        rows.append(jnp.sum((cot * o_ref[:, lanes].astype(F32)).T, axis=0, keepdims=True))
        cot = cot.astype(BF)
        for x in range(4):
            out_ref[x, h * TOK : (h + 1) * TOK, :] = q_ref[:, lanes]
            out_ref[x, COLS + h * TOK : COLS + (h + 1) * TOK, :] = cot
    delta = jnp.concatenate(rows, axis=0)
    high = delta.astype(BF).astype(F32)
    low = delta - high
    tail = jnp.concatenate(
        [high, low, seg_ref[...].astype(F32), jnp.zeros((7, TOK), F32)], axis=0
    ).astype(BF)
    for x in range(4):
        out_ref[x, 2 * COLS :, :] = tail


def pack_keys(own_ref, one_ref, two_ref, seg_ref, out_ref):
    tail = jnp.concatenate(
        [seg_ref[...].astype(F32), jnp.zeros((15, TOK), F32)], axis=0
    ).astype(BF)
    for s, ref in enumerate((own_ref, one_ref, two_ref)):
        for half in range(2):
            part = ref[half * HALF : (half + 1) * HALF, :]
            for r in range(GROUP):
                out_ref[2 * r + half, s * HALF : (s + 1) * HALF, :] = part
    for i in range(2 * GROUP):
        out_ref[i, SLOTS * HALF :, :] = tail


def position():
    return (
        lax.axis_index("zg"),
        lax.axis_index("zr"),
        lax.axis_index("xh"),
        lax.axis_index("core"),
        lax.axis_index("pair"),
    )


def slot_count(zg):
    return jnp.where(zg == 3, 1, zg + 1)


def key_block(kv_ref, kind, s):
    first = s * HALF if isinstance(s, int) else pl.multiple_of(s * HALF, HALF)
    return kv_ref[:, kind, pl.ds(first, HALF), :].reshape(KEYS, HEAD)


def key_segments(kv_ref, pair, turn_ref, seg_ref):
    for r in range(GROUP):
        row = kv_ref[r, 0, SLOTS * HALF :, :].astype(F32)[0:1]
        turn_ref[...] = jnp.broadcast_to(row, (TOK, TOK)).T
        seg_ref[r * HALF : (r + 1) * HALF, :] = turn_ref[
            pl.ds(pl.multiple_of(pair * HALF, HALF), HALF), :
        ]


def allowed_pairs(place, query_seg, hx, from_core, seg_ref):
    zg, zr, xh, core, pair = place
    row = lax.broadcasted_iota(jnp.int32, (KEYS, TOK), 0)
    key_pos = (row // HALF) * 512 + row % HALF + ((2 * xh + core) * TOK + pair * HALF)
    lane = lax.broadcasted_iota(jnp.int32, (KEYS, TOK), 1)
    query_pos = lane + (zr * 512 + (2 * hx + from_core) * TOK)
    return (key_pos <= query_pos) & (seg_ref[...] == query_seg)


def tiled(mask):
    return jnp.concatenate([mask] * HEADS, axis=1)


def by_count(place, body):
    count = slot_count(place[0])
    for n in (1, 2, 3):

        @pl.when(count == n)
        def _(n=n):
            body(n)


def flat(rows):
    return jnp.concatenate([rows[h : h + 1] for h in range(HEADS)], axis=1)


def row_sums(same_ref, other_ref, kv_ref, out_ref, turn_ref, seg_ref):
    place = position()
    core, pair = place[3:]
    key_segments(kv_ref, pair, turn_ref, seg_ref)

    def body(n):
        def sources(hx, _):
            for other, q_ref in enumerate((same_ref, other_ref)):
                from_core = (1 - core) if other else core
                segs = q_ref[2 * hx, 2 * COLS :, :].astype(F32)[8:9]
                allowed = tiled(allowed_pairs(place, segs, hx, from_core, seg_ref))
                for p in range(2):
                    x = 2 * hx + p
                    q = q_ref[x, :COLS, :]
                    scores = [dot(key_block(kv_ref, 0, j), q, NT) * SCALE2 for j in range(n)]
                    scores[0] = jnp.where(allowed, scores[0], NEGATIVE)
                    top = jnp.full((1, COLS), 0.1 * NEGATIVE, F32)
                    for s in scores:
                        top = jnp.maximum(top, jnp.max(s, axis=0, keepdims=True))
                    total = jnp.zeros((1, COLS), F32)
                    for s in scores:
                        total += jnp.sum(jnp.exp2(s - top), axis=0, keepdims=True)
                    norm = jnp.maximum(top + jnp.log2(total), NEGATIVE)
                    for h in range(HEADS):
                        piece = jnp.broadcast_to(norm[:, h * TOK : (h + 1) * TOK], (8, TOK))
                        out_ref[:, from_core, x, h : h + 1, :] = piece.reshape(8, 1, TOK)
            return 0

        lax.fori_loop(0, 2, sources, 0)

    by_count(place, body)


def gradients(
    same_ref, other_ref, kv_ref, norm_ref,
    dq_same_ref, dq_other_ref, dkv_ref,
    turn_ref, seg_ref, log_ref, turned_ref, dk_ref, dv_ref,
):
    place = position()
    core, pair = place[3:]
    key_segments(kv_ref, pair, turn_ref, seg_ref)
    norms = norm_ref[...]
    top = jnp.max(norms, axis=0)
    log_ref[...] = top + jnp.log2(jnp.sum(jnp.exp2(norms - top[None]), axis=0)) - LOG_SCALE
    for s in range(SLOTS):
        turned_ref[s] = key_block(kv_ref, 0, s).astype(F32).T.astype(BF)
    dk_ref[...] = jnp.zeros_like(dk_ref)
    dv_ref[...] = jnp.zeros_like(dv_ref)

    def body(n):
        for other, q_ref, dq_ref in ((1, other_ref, dq_other_ref), (0, same_ref, dq_same_ref)):
            from_core = (1 - core) if other else core

            def sources(hx, _, q_ref=q_ref, dq_ref=dq_ref, from_core=from_core):
                segs = q_ref[2 * hx, 2 * COLS :, :].astype(F32)[8:9]
                allowed = tiled(allowed_pairs(place, segs, hx, from_core, seg_ref))
                for p in range(2):
                    x = 2 * hx + p
                    q = q_ref[x, :COLS, :]
                    cot = q_ref[x, COLS : 2 * COLS, :]
                    tail = q_ref[x, 2 * COLS :, :].astype(F32)
                    delta = flat(tail[0:HEADS] + tail[HEADS : 2 * HEADS])
                    norm = flat(log_ref[from_core, x])
                    dq = None
                    for j in range(n):
                        s = dot(key_block(kv_ref, 0, j), q, NT)
                        prob = jnp.exp2(s * SCALE2 - norm)
                        if j == 0:
                            prob = jnp.where(allowed, prob, 0.0)
                        dprob = dot(key_block(kv_ref, 1, j), cot, NT)
                        dscore = (prob * (dprob - delta)).astype(BF)
                        dk_ref[j] += dot(dscore, q, NN)
                        dv_ref[j] += dot(prob.astype(BF), cot, NN)
                        part = dot(turned_ref[j], dscore, NN)
                        dq = part if dq is None else dq + part
                    dq_ref[x] = dq.astype(BF)
                return 0

            lax.fori_loop(0, 2, sources, 0)

    by_count(place, body)

    for s in range(SLOTS):
        for r in range(GROUP):
            rows = slice(r * HALF, (r + 1) * HALF)
            dkv_ref[2 * r, s] = dk_ref[s, rows, :].astype(BF)
            dkv_ref[2 * r + 1, s] = (dv_ref[s, rows, :] * (1.0 / SCALE)).astype(BF)


def add_parts(dkv_ref, same_ref, other_ref, own_ref, one_ref, two_ref, dq_ref):
    for s, ref in enumerate((own_ref, one_ref, two_ref)):
        for half in range(2):
            total = dkv_ref[half, s].astype(F32)
            for r in range(1, GROUP):
                total += dkv_ref[2 * r + half, s].astype(F32)
            ref[half * HALF : (half + 1) * HALF, :] = total.astype(ref.dtype)
    dq_ref[...] = (same_ref[...].astype(F32) + other_ref[...].astype(F32)).astype(BF)


def finish(dq_ref, own_ref, one_ref, two_ref, out_q_ref, out_kv_ref):
    total = dq_ref[0].astype(F32)
    for x in range(1, 4):
        total += dq_ref[x].astype(F32)
    for h in range(HEADS):
        lanes = slice(h * HEAD, (h + 1) * HEAD)
        out_q_ref[:, lanes] = total[:, lanes].T.astype(BF)
    out_kv_ref[...] = (
        own_ref[...] + one_ref[...].astype(F32) + two_ref[...].astype(F32)
    ).astype(BF)


def per_device(queries, stored_key_value, out_grad, attn_out, segment_ids, loss_mask):
    seg = segment_ids.reshape(1, TOK)
    mask = loss_mask.reshape(1, TOK)
    swap = [(0, 1), (1, 0)]

    one = lax.ppermute(stored_key_value, "zg", [(0, 1), (1, 2)])
    two = lax.ppermute(stored_key_value, "zg", [(0, 2)])
    packed = call(pack_queries, "pack_queries", shape((4, Q_ROWS, HEAD), BF))(
        queries, out_grad, attn_out, seg, mask
    )
    same = lax.all_to_all(packed, X_AXES, 0, 0, tiled=True)
    other = lax.ppermute(same, "core", swap)
    kv_packed = call(
        pack_keys, "pack_keys", shape((2 * GROUP, KV_ROWS, HEAD), BF), resident=(1, 2)
    )(
        stored_key_value, one, two, seg
    )
    kv = lax.all_to_all(kv_packed, ("zr", "pair"), 0, 0, tiled=True)
    kv = kv.reshape(GROUP, 2, KV_ROWS, HEAD)

    segs = [pltpu.VMEM((TOK, TOK), F32), pltpu.VMEM((KEYS, TOK), F32)]
    norms = call(
        row_sums, "row_sums", shape((8, 2, 4, HEADS, TOK), F32), segs, resident=(0, 1, 2)
    )(same, other, kv)
    norms = lax.all_to_all(norms, PLANE, 0, 0, tiled=True)

    dq_same, dq_other, dkv = call(
        gradients,
        "gradients",
        (
            shape((4, HEAD, COLS), BF),
            shape((4, HEAD, COLS), BF),
            shape((2 * GROUP, SLOTS, HALF, HEAD), BF),
        ),
        segs
        + [
            pltpu.VMEM((2, 4, HEADS, TOK), F32),
            pltpu.VMEM((SLOTS, HEAD, KEYS), BF),
            pltpu.VMEM((SLOTS, KEYS, HEAD), F32),
            pltpu.VMEM((SLOTS, KEYS, HEAD), F32),
        ],
        resident=(0, 1, 2, 3),
    )(same, other, kv, norms)
    dq_other = lax.ppermute(dq_other, "core", swap)
    dkv = lax.all_to_all(dkv, ("zr", "pair"), 0, 0, tiled=True)

    own, one, two, dq = call(
        add_parts,
        "add_parts",
        (
            shape((TOK, HEAD), F32),
            shape((TOK, HEAD), BF),
            shape((TOK, HEAD), BF),
            shape((4, HEAD, COLS), BF),
        ),
        resident=(0, 1, 2),
    )(dkv, dq_same, dq_other)
    one = lax.ppermute(one, "zg", [(1, 0), (2, 1)])
    two = lax.ppermute(two, "zg", [(2, 0)])
    dq = lax.all_to_all(dq, X_AXES, 0, 0, tiled=True)
    return call(
        finish,
        "finish",
        (shape((TOK, HEADS * HEAD), BF), shape((TOK, HEAD), BF)),
        resident=(0, 1, 2, 3),
    )(dq, own, one, two)


def solution(mesh):
    fine = Mesh(
        mesh.devices.reshape(4, 4, 2, 2, 4, 2), ("zg", "zr", "xh", "core", "tp", "pair")
    )
    rows = ("zg", "zr", "xh", "core")
    wide = P(rows, ("tp", "pair"))
    return jax.shard_map(
        per_device,
        mesh=fine,
        in_specs=(wide, wide, wide, wide, P(rows), P(rows)),
        out_specs=(wide, wide),
        check_vma=False,
    )
```

```python
import functools
import math

import jax
import jax.numpy as jnp
from jax import lax
from jax.experimental import pallas as pl
from jax.experimental.pallas import tpu as pltpu
from jax.sharding import Mesh, PartitionSpec as P

BF = jnp.bfloat16
F32 = jnp.float32
NEGATIVE = -1e30
TOK = 128
HEAD = 128
HEADS = 4
COLS = HEADS * TOK
GROUP = 4
SLOTS = 3
HALF = TOK // 2
KEYS = GROUP * HALF
Q_ROWS = 2 * COLS + 16
KV_ROWS = SLOTS * HALF + 16
FULL = (2, 4, SLOTS, KEYS, COLS)
SCALE = 1.0 / math.sqrt(HEAD)
SCALE2 = SCALE * math.log2(math.e)
LOG_SCALE = math.log2(SCALE)
X_AXES = ("xh", "pair")
Z_AXES = ("zg", "zr")
MIRROR = [(r, 11 - r) for r in range(4)]
PLANE = ("xh", "core", "pair")
NT = (((1,), (1,)), ((), ()))
NN = (((1,), (0,)), ((), ()))
VMEM_LIMIT = 40 * 1024 * 1024


def dot(a, b, dims):
    return lax.dot_general(a, b, dims, preferred_element_type=F32)


def call(kernel, name, out_shape, scratch=(), near=(), far=(), far_out=()):
    def bound(*args):
        specs = [
            pl.BlockSpec(memory_space=pltpu.HBM if i in far else pltpu.VMEM)
            for i in range(len(args))
        ]
        outs = out_shape if isinstance(out_shape, tuple) else (out_shape,)
        out_specs = tuple(
            pl.BlockSpec(memory_space=pltpu.HBM if i in far_out else pltpu.VMEM)
            for i in range(len(outs))
        )
        kept = [
            pltpu.with_memory_space_constraint(a, pltpu.VMEM if i in near else pltpu.HBM)
            for i, a in enumerate(args)
        ]
        run = pl.pallas_call(
            kernel,
            out_shape=outs,
            in_specs=specs,
            out_specs=out_specs,
            scratch_shapes=scratch,
            name=name,
            compiler_params=pltpu.CompilerParams(vmem_limit_bytes=VMEM_LIMIT),
        )
        got = run(*kept)
        return got if isinstance(out_shape, tuple) else got[0]

    return bound


def shape(dims, dtype):
    return jax.ShapeDtypeStruct(dims, dtype)


def pack_queries(
    q_hbm, g_hbm, o_hbm, seg_hbm, mask_hbm, out_ref, q_ref, g_ref, o_ref, seg_ref, mask_ref, sems
):
    copies = [
        pltpu.make_async_copy(far, ref, sems.at[i])
        for i, (far, ref) in enumerate(
            (
                (mask_hbm, mask_ref),
                (g_hbm, g_ref),
                (o_hbm, o_ref),
                (q_hbm, q_ref),
                (seg_hbm, seg_ref),
            )
        )
    ]
    for copy in copies:
        copy.start()
    for copy in copies:
        copy.wait()
    mask = jnp.broadcast_to(mask_ref[...].astype(F32), (TOK, TOK)).T
    rows = []
    for h in range(HEADS):
        lanes = slice(h * HEAD, (h + 1) * HEAD)
        cot = g_ref[:, lanes].astype(F32) * mask
        rows.append(jnp.sum((cot * o_ref[:, lanes].astype(F32)).T, axis=0, keepdims=True))
        cot = cot.astype(BF)
        for x in range(4):
            out_ref[x, h * TOK : (h + 1) * TOK, :] = q_ref[:, lanes]
            out_ref[x, COLS + h * TOK : COLS + (h + 1) * TOK, :] = cot
    delta = jnp.concatenate(rows, axis=0)
    high = delta.astype(BF).astype(F32)
    low = delta - high
    tail = jnp.concatenate(
        [high, low, seg_ref[...].astype(F32), jnp.zeros((7, TOK), F32)], axis=0
    ).astype(BF)
    for x in range(4):
        out_ref[x, 2 * COLS :, :] = tail


def pack_keys(own_ref, one_ref, two_ref, seg_ref, out_ref):
    tail = jnp.concatenate(
        [seg_ref[...].astype(F32), jnp.zeros((15, TOK), F32)], axis=0
    ).astype(BF)
    for s, ref in enumerate((own_ref, one_ref, two_ref)):
        for half in range(2):
            part = ref[half * HALF : (half + 1) * HALF, :]
            for r in range(GROUP):
                out_ref[2 * r + half, s * HALF : (s + 1) * HALF, :] = part
    for i in range(2 * GROUP):
        out_ref[i, SLOTS * HALF :, :] = tail


def position():
    return (
        lax.axis_index("zg"),
        lax.axis_index("zr"),
        lax.axis_index("xh"),
        lax.axis_index("core"),
        lax.axis_index("pair"),
    )


def slot_count(zg):
    return jnp.where(zg == 3, 1, zg + 1)


def key_block(kv_ref, kind, s):
    first = s * HALF if isinstance(s, int) else pl.multiple_of(s * HALF, HALF)
    return kv_ref[:, kind, pl.ds(first, HALF), :].reshape(KEYS, HEAD)


def key_segments(kv_ref, pair, turn_ref, seg_ref):
    for r in range(GROUP):
        row = kv_ref[r, 0, SLOTS * HALF :, :].astype(F32)[0:1]
        turn_ref[...] = jnp.broadcast_to(row, (TOK, TOK)).T
        seg_ref[r * HALF : (r + 1) * HALF, :] = turn_ref[
            pl.ds(pl.multiple_of(pair * HALF, HALF), HALF), :
        ]


def allowed_pairs(place, query_seg, hx, from_core, seg_ref):
    zg, zr, xh, core, pair = place
    row = lax.broadcasted_iota(jnp.int32, (KEYS, TOK), 0)
    key_pos = (row // HALF) * 512 + row % HALF + ((2 * xh + core) * TOK + pair * HALF)
    lane = lax.broadcasted_iota(jnp.int32, (KEYS, TOK), 1)
    query_pos = lane + (zr * 512 + (2 * hx + from_core) * TOK)
    return (key_pos <= query_pos) & (seg_ref[...] == query_seg)


def tiled(mask):
    return jnp.concatenate([mask] * HEADS, axis=1)


def by_count(place, body):
    count = slot_count(place[0])
    for n in (1, 2, 3):

        @pl.when(count == n)
        def _(n=n):
            body(n)


def flat(rows):
    return jnp.concatenate([rows[h : h + 1] for h in range(HEADS)], axis=1)


def blocks(from_ref, to_ref, n, other, x, sems):
    return pltpu.make_async_copy(
        from_ref.at[other, x, pl.ds(0, n)], to_ref.at[other, x, pl.ds(0, n)], sems.at[other, x]
    )


def row_sums(
    same_ref, other_ref, kv_ref, out_ref, top_ref, prob_hbm, turn_ref, seg_ref, prob_ref, sems
):
    place = position()
    core, pair = place[3:]
    key_segments(kv_ref, pair, turn_ref, seg_ref)

    def body(n):
        def sources(hx, _):
            for other, q_ref in enumerate((same_ref, other_ref)):
                from_core = (1 - core) if other else core
                segs = q_ref[2 * hx, 2 * COLS :, :].astype(F32)[8:9]
                allowed = tiled(allowed_pairs(place, segs, hx, from_core, seg_ref))
                for p in range(2):
                    x = 2 * hx + p
                    q = q_ref[x, :COLS, :]
                    scores = [dot(key_block(kv_ref, 0, j), q, NT) * SCALE2 for j in range(n)]
                    scores[0] = jnp.where(allowed, scores[0], NEGATIVE)
                    top = jnp.full((1, COLS), 0.1 * NEGATIVE, F32)
                    for s in scores:
                        top = jnp.maximum(top, jnp.max(s, axis=0, keepdims=True))
                    total = jnp.zeros((1, COLS), F32)
                    for j, s in enumerate(scores):
                        prob = jnp.exp2(s - top)
                        total += jnp.sum(prob, axis=0, keepdims=True)
                        prob_ref[other, x, j] = prob.astype(BF)
                    norm = jnp.maximum(top + jnp.log2(total), NEGATIVE)
                    for h in range(HEADS):
                        lanes = slice(h * TOK, (h + 1) * TOK)
                        top_ref[other, x, h : h + 1, :] = top[:, lanes]
                        piece = jnp.broadcast_to(norm[:, lanes], (8, TOK))
                        out_ref[:, from_core, x, h : h + 1, :] = piece.reshape(8, 1, TOK)
                    blocks(prob_ref, prob_hbm, n, other, x, sems).start()
            return 0

        lax.fori_loop(0, 2, sources, 0)
        for other in range(2):
            for x in range(4):
                blocks(prob_ref, prob_hbm, n, other, x, sems).wait()

    by_count(place, body)


def raw_scores(
    same_ref, other_ref, kv_ref, prob_hbm, score_hbm, prob_ref, score_ref, in_sems, out_sems
):
    def body(n):
        for x in range(4):
            for other in range(2):
                blocks(prob_hbm, prob_ref, n, other, x, in_sems).start()

        def sources(x, _):
            for other, g_ref in enumerate((same_ref, other_ref)):
                cot = g_ref[x, COLS : 2 * COLS, :]
                tail = g_ref[x, 2 * COLS :, :].astype(F32)
                delta = flat(tail[0:HEADS] + tail[HEADS : 2 * HEADS])
                blocks(prob_hbm, prob_ref, n, other, x, in_sems).wait()
                for j in range(n):
                    dprob = dot(key_block(kv_ref, 1, j), cot, NT)
                    score_ref[other, x, j] = (
                        prob_ref[other, x, j].astype(F32) * (dprob - delta)
                    ).astype(BF)
                blocks(score_ref, score_hbm, n, other, x, out_sems).start()
            return 0

        lax.fori_loop(0, 4, sources, 0)
        for x in range(4):
            for other in range(2):
                blocks(score_ref, score_hbm, n, other, x, out_sems).wait()

    by_count(position(), body)


def over_sources(left_ref, right_ref, j):
    total = None
    for other in range(2):
        for x in range(4):
            part = dot(left_ref[other, x, j], right_ref[other, x], NN)
            total = part if total is None else total + part
    return total


def key_gradients(
    same_ref, other_ref, norm_ref, top_ref, prob_hbm, score_hbm,
    dkv_ref, weight_ref, q_ref, g_ref, prob_ref, score_ref, sems,
):
    place = position()
    core = place[3]
    count = slot_count(place[0])

    def fetch(j, kind):
        far, near = ((score_hbm, score_ref), (prob_hbm, prob_ref))[kind]
        return pltpu.make_async_copy(far.at[:, :, j], near.at[:, :, j], sems.at[j, kind])

    for j in range(SLOTS):

        @pl.when(j < count)
        def _(j=j):
            fetch(j, 0).start()
            fetch(j, 1).start()

    norms = norm_ref[...]
    top = jnp.max(norms, axis=0)
    log_norm = top + jnp.log2(jnp.sum(jnp.exp2(norms - top[None]), axis=0))
    own = jnp.where(core == 0, log_norm[0], log_norm[1])
    far = jnp.where(core == 0, log_norm[1], log_norm[0])
    weight_ref[0] = jnp.exp2(top_ref[0] - own)
    weight_ref[1] = jnp.exp2(top_ref[1] - far)

    def scaled(x, _):
        for other, source_ref in enumerate((same_ref, other_ref)):
            weights = weight_ref[other, x]
            for h in range(HEADS):
                rows = slice(h * TOK, (h + 1) * TOK)
                below = slice(COLS + h * TOK, COLS + (h + 1) * TOK)
                by_row = jnp.broadcast_to(weights[h : h + 1], (TOK, TOK)).T
                q = source_ref[x, rows, :].astype(F32) * (by_row * SCALE)
                q_ref[other, x, rows, :] = q.astype(BF)
                g_ref[other, x, rows, :] = (
                    source_ref[x, below, :].astype(F32) * by_row
                ).astype(BF)
        return 0

    lax.fori_loop(0, 4, scaled, 0)

    def body(n):
        for s in range(SLOTS):
            for kind, left_ref, right_ref in ((0, score_ref, q_ref), (1, prob_ref, g_ref)):
                if s < n:
                    fetch(s, kind).wait()
                    total = over_sources(left_ref, right_ref, s).astype(BF)
                else:
                    total = jnp.zeros((KEYS, HEAD), BF)
                for r in range(GROUP):
                    dkv_ref[2 * r + kind, s * HALF : (s + 1) * HALF, :] = total[
                        r * HALF : (r + 1) * HALF
                    ]

    by_count(place, body)


def query_gradients(
    kv_ref, score_hbm, weight_ref, same_ref, other_ref, turned_ref, score_ref, sems
):

    def body(n):
        for x in range(4):
            for other in (1, 0):
                blocks(score_hbm, score_ref, n, other, x, sems).start()
        for s in range(n):
            turned_ref[s] = key_block(kv_ref, 0, s).astype(F32).T.astype(BF)

        def sources(x, _):
            for other, dq_ref in ((1, other_ref), (0, same_ref)):
                blocks(score_hbm, score_ref, n, other, x, sems).wait()
                dq = dot(turned_ref[0], score_ref[other, x, 0], NN)
                for j in range(1, n):
                    dq += dot(turned_ref[j], score_ref[other, x, j], NN)
                dq_ref[x] = (dq * (flat(weight_ref[other, x]) * SCALE)).astype(BF)
            return 0

        lax.fori_loop(0, 4, sources, 0)

    by_count(position(), body)


def sum_keys(dkv_ref, own_ref, one_ref, two_ref):
    for s, ref in enumerate((own_ref, one_ref, two_ref)):
        for half in range(2):
            total = dkv_ref[half, s * HALF : (s + 1) * HALF, :].astype(F32)
            for r in range(1, GROUP):
                total += dkv_ref[2 * r + half, s * HALF : (s + 1) * HALF, :].astype(F32)
            ref[half * HALF : (half + 1) * HALF, :] = total.astype(ref.dtype)


def sum_cores(same_ref, other_ref, out_ref):
    out_ref[...] = (same_ref[...].astype(F32) + other_ref[...].astype(F32)).astype(BF)


def finish(dq_ref, own_ref, one_ref, two_ref, out_q_ref, out_kv_ref):
    total = dq_ref[0].astype(F32)
    for x in range(1, 4):
        total += dq_ref[x].astype(F32)
    for h in range(HEADS):
        lanes = slice(h * HEAD, (h + 1) * HEAD)
        out_q_ref[:, lanes] = total[:, lanes].T.astype(BF)
    out_kv_ref[...] = (
        own_ref[...] + one_ref[...].astype(F32) + two_ref[...].astype(F32)
    ).astype(BF)


def local_kernels(same, other, kv, exchange):
    norms, tops, prob = call(
        row_sums,
        "row_sums",
        (
            shape((8, 2, 4, HEADS, TOK), F32),
            pltpu.VMEM((2, 4, HEADS, TOK), F32),
            pltpu.HBM(FULL, BF),
        ),
        [
            pltpu.VMEM((TOK, TOK), F32),
            pltpu.VMEM((KEYS, TOK), F32),
            pltpu.VMEM(FULL, BF),
            pltpu.SemaphoreType.DMA((2, 4)),
        ],
        near=range(3),
        far_out=(2,),
    )(same, other, kv)
    norms = exchange(norms)
    scores = call(
        raw_scores,
        "raw_scores",
        pltpu.HBM(FULL, BF),
        [
            pltpu.VMEM(FULL, BF),
            pltpu.VMEM(FULL, BF),
            pltpu.SemaphoreType.DMA((2, 4)),
            pltpu.SemaphoreType.DMA((2, 4)),
        ],
        near=range(3),
        far=(3,),
        far_out=(0,),
    )(same, other, kv, prob)
    dkv, weights = call(
        key_gradients,
        "key_gradients",
        (
            shape((2 * GROUP, SLOTS * HALF, HEAD), BF),
            pltpu.VMEM((2, 4, HEADS, TOK), F32),
        ),
        [
            pltpu.VMEM((2, 4, COLS, HEAD), BF),
            pltpu.VMEM((2, 4, COLS, HEAD), BF),
            pltpu.VMEM(FULL, BF),
            pltpu.VMEM(FULL, BF),
            pltpu.SemaphoreType.DMA((SLOTS, 2)),
        ],
        near=range(4),
        far=(4, 5),
    )(same, other, norms, tops, prob, scores)
    dq_same, dq_other = call(
        query_gradients,
        "query_gradients",
        (pltpu.VMEM((4, HEAD, COLS), BF), shape((4, HEAD, COLS), BF)),
        [
            pltpu.VMEM((SLOTS, HEAD, KEYS), BF),
            pltpu.VMEM(FULL, BF),
            pltpu.SemaphoreType.DMA((2, 4)),
        ],
        near=(0, 2),
        far=(1,),
    )(kv, scores, weights)
    return dkv, dq_same, dq_other


def per_device(queries, stored_key_value, out_grad, attn_out, segment_ids, loss_mask):
    seg = segment_ids.reshape(1, TOK)
    mask = loss_mask.reshape(1, TOK)
    swap = [(0, 1), (1, 0)]

    two = lax.ppermute(stored_key_value, Z_AXES, MIRROR)
    one = lax.ppermute(stored_key_value, "zg", [(0, 1), (1, 2)])
    wide = pltpu.VMEM((TOK, HEADS * HEAD), BF)
    line = pltpu.VMEM((1, TOK), jnp.int32)
    packed = call(
        pack_queries,
        "pack_queries",
        shape((4, Q_ROWS, HEAD), BF),
        [wide, wide, wide, line, line, pltpu.SemaphoreType.DMA((5,))],
        far=range(5),
    )(queries, out_grad, attn_out, seg, mask)
    same = lax.all_to_all(packed, X_AXES, 0, 0, tiled=True)
    other = lax.ppermute(same, "core", swap)
    kv = call(pack_keys, "pack_keys", shape((2 * GROUP, KV_ROWS, HEAD), BF), near=(1, 2))(
        stored_key_value, one, two, seg
    )
    kv = lax.all_to_all(kv, ("zr", "pair"), 0, 0, tiled=True).reshape(GROUP, 2, KV_ROWS, HEAD)

    dkv, dq_same, dq_other = local_kernels(
        same, other, kv, lambda norms: lax.all_to_all(norms, PLANE, 0, 0, tiled=True)
    )
    dkv = lax.all_to_all(dkv, ("zr", "pair"), 0, 0, tiled=True)
    dq_other = lax.ppermute(dq_other, "core", swap)
    own, one, two = call(
        sum_keys,
        "sum_keys",
        (pltpu.VMEM((TOK, HEAD), F32), shape((TOK, HEAD), BF), shape((TOK, HEAD), BF)),
        near=(0,),
    )(dkv)
    one = lax.ppermute(one, "zg", [(1, 0), (2, 1)])
    two = lax.ppermute(two, Z_AXES, [(b, a) for a, b in MIRROR])
    dq = call(sum_cores, "sum_cores", shape((4, HEAD, COLS), BF), near=(0, 1))(dq_same, dq_other)
    dq = lax.all_to_all(dq, X_AXES, 0, 0, tiled=True)
    return call(
        finish,
        "finish",
        (shape((TOK, HEADS * HEAD), BF), shape((TOK, HEAD), BF)),
        near=range(4),
    )(dq, own, one, two)


def solution(mesh):
    fine = Mesh(
        mesh.devices.reshape(4, 4, 2, 2, 4, 2), ("zg", "zr", "xh", "core", "tp", "pair")
    )
    rows = ("zg", "zr", "xh", "core")
    wide = P(rows, ("tp", "pair"))
    return jax.shard_map(
        per_device,
        mesh=fine,
        in_specs=(wide, wide, wide, wide, P(rows), P(rows)),
        out_specs=(wide, wide),
        check_vma=False,
    )
```

```python
import functools
import math

import jax
import jax.numpy as jnp
from jax import lax
from jax.experimental import pallas as pl
from jax.experimental.pallas import tpu as pltpu
from jax.sharding import Mesh, PartitionSpec as P

BF = jnp.bfloat16
F32 = jnp.float32
NEGATIVE = -1e30
TOK = 128
HEAD = 128
HEADS = 4
COLS = HEADS * TOK
GROUP = 4
SLOTS = 3
HALF = TOK // 2
KEYS = GROUP * HALF
Q_ROWS = 2 * COLS + 16
KV_ROWS = SLOTS * HALF + 16
FULL = (2, 4, SLOTS, KEYS, COLS)
SCALE = 1.0 / math.sqrt(HEAD)
SCALE2 = SCALE * math.log2(math.e)
LOG_SCALE = math.log2(SCALE)
X_AXES = ("xh", "pair")
Z_AXES = ("zg", "zr")
FAR = [(r, 8 + (r + 2) % 4) for r in range(4)]
PLANE = ("xh", "core", "pair")
NT = (((1,), (1,)), ((), ()))
NN = (((1,), (0,)), ((), ()))
VMEM_LIMIT = 40 * 1024 * 1024
LONG = pl.CostEstimate(flops=40_000_000_000, bytes_accessed=120_000_000, transcendentals=0)


def dot(a, b, dims):
    return lax.dot_general(a, b, dims, preferred_element_type=F32)


def call(kernel, name, out_shape, scratch=(), near=(), far=(), far_out=(), cost=None):
    def bound(*args):
        specs = [
            pl.BlockSpec(memory_space=pltpu.HBM if i in far else pltpu.VMEM)
            for i in range(len(args))
        ]
        outs = out_shape if isinstance(out_shape, tuple) else (out_shape,)
        out_specs = tuple(
            pl.BlockSpec(memory_space=pltpu.HBM if i in far_out else pltpu.VMEM)
            for i in range(len(outs))
        )
        kept = [
            pltpu.with_memory_space_constraint(a, pltpu.VMEM if i in near else pltpu.HBM)
            for i, a in enumerate(args)
        ]
        run = pl.pallas_call(
            kernel,
            out_shape=outs,
            in_specs=specs,
            out_specs=out_specs,
            scratch_shapes=scratch,
            name=name,
            cost_estimate=cost,
            compiler_params=pltpu.CompilerParams(vmem_limit_bytes=VMEM_LIMIT),
        )
        got = run(*kept)
        return got if isinstance(out_shape, tuple) else got[0]

    return bound


def shape(dims, dtype):
    return jax.ShapeDtypeStruct(dims, dtype)


def pack_queries(
    q_hbm, g_hbm, o_hbm, seg_hbm, mask_hbm, out_ref, q_ref, g_ref, o_ref, seg_ref, mask_ref, sems
):
    copies = [
        pltpu.make_async_copy(far, ref, sems.at[i])
        for i, (far, ref) in enumerate(
            (
                (q_hbm, q_ref),
                (mask_hbm, mask_ref),
                (seg_hbm, seg_ref),
                (g_hbm, g_ref),
                (o_hbm, o_ref),
            )
        )
    ]
    for copy in copies:
        copy.start()
    copies[0].wait()
    for h in range(HEADS):
        for x in range(4):
            out_ref[x, h * TOK : (h + 1) * TOK, :] = q_ref[:, h * HEAD : (h + 1) * HEAD]
    for copy in copies[1:]:
        copy.wait()
    mask = jnp.broadcast_to(mask_ref[...].astype(F32), (TOK, TOK)).T
    rows = []
    for h in range(HEADS):
        lanes = slice(h * HEAD, (h + 1) * HEAD)
        cot = g_ref[:, lanes].astype(F32) * mask
        rows.append(jnp.sum((cot * o_ref[:, lanes].astype(F32)).T, axis=0, keepdims=True))
        cot = cot.astype(BF)
        for x in range(4):
            out_ref[x, COLS + h * TOK : COLS + (h + 1) * TOK, :] = cot
    delta = jnp.concatenate(rows, axis=0)
    high = delta.astype(BF).astype(F32)
    low = delta - high
    tail = jnp.concatenate(
        [high, low, seg_ref[...].astype(F32), jnp.zeros((7, TOK), F32)], axis=0
    ).astype(BF)
    for x in range(4):
        out_ref[x, 2 * COLS :, :] = tail


def pack_keys(own_ref, two_ref, one_ref, seg_ref, out_ref):
    tail = jnp.concatenate(
        [seg_ref[...].astype(F32), jnp.zeros((15, TOK), F32)], axis=0
    ).astype(BF)
    for s, ref in enumerate((own_ref, one_ref, two_ref)):
        for half in range(2):
            part = ref[half * HALF : (half + 1) * HALF, :]
            for r in range(GROUP):
                out_ref[2 * r + half, s * HALF : (s + 1) * HALF, :] = part
    for i in range(2 * GROUP):
        out_ref[i, SLOTS * HALF :, :] = tail


def position():
    return (
        lax.axis_index("zg"),
        lax.axis_index("zr"),
        lax.axis_index("xh"),
        lax.axis_index("core"),
        lax.axis_index("pair"),
    )


def slot_count(zg):
    return jnp.where(zg == 3, 1, zg + 1)


def key_block(kv_ref, kind, s):
    first = s * HALF if isinstance(s, int) else pl.multiple_of(s * HALF, HALF)
    return kv_ref[:, kind, pl.ds(first, HALF), :].reshape(KEYS, HEAD)


def key_segments(kv_ref, pair, turn_ref, seg_ref):
    for r in range(GROUP):
        row = kv_ref[r, 0, SLOTS * HALF :, :].astype(F32)[0:1]
        turn_ref[...] = jnp.broadcast_to(row, (TOK, TOK)).T
        seg_ref[r * HALF : (r + 1) * HALF, :] = turn_ref[
            pl.ds(pl.multiple_of(pair * HALF, HALF), HALF), :
        ]


def allowed_pairs(place, query_seg, hx, from_core, seg_ref):
    zg, zr, xh, core, pair = place
    row = lax.broadcasted_iota(jnp.int32, (KEYS, TOK), 0)
    key_pos = (row // HALF) * 512 + row % HALF + ((2 * xh + core) * TOK + pair * HALF)
    lane = lax.broadcasted_iota(jnp.int32, (KEYS, TOK), 1)
    query_pos = lane + (zr * 512 + (2 * hx + from_core) * TOK)
    return (key_pos <= query_pos) & (seg_ref[...] == query_seg)


def tiled(mask):
    return jnp.concatenate([mask] * HEADS, axis=1)


def by_count(place, body):
    count = slot_count(place[0])
    for n in (1, 2, 3):

        @pl.when(count == n)
        def _(n=n):
            body(n)


def flat(rows):
    return jnp.concatenate([rows[h : h + 1] for h in range(HEADS)], axis=1)


def blocks(from_ref, to_ref, n, other, x, sems):
    return pltpu.make_async_copy(
        from_ref.at[other, x, pl.ds(0, n)], to_ref.at[other, x, pl.ds(0, n)], sems.at[other, x]
    )


def row_sums(
    same_ref, other_ref, kv_ref, out_ref, top_ref, prob_hbm, turn_ref, seg_ref, prob_ref, sems
):
    place = position()
    core, pair = place[3:]
    key_segments(kv_ref, pair, turn_ref, seg_ref)

    def body(n):
        def sources(hx):
            for other, q_ref in enumerate((same_ref, other_ref)):
                from_core = (1 - core) if other else core
                segs = q_ref[2 * hx, 2 * COLS :, :].astype(F32)[8:9]
                allowed = tiled(allowed_pairs(place, segs, hx, from_core, seg_ref))
                for p in range(2):
                    x = 2 * hx + p
                    q = q_ref[x, :COLS, :]
                    scores = [dot(key_block(kv_ref, 0, j), q, NT) * SCALE2 for j in range(n)]
                    scores[0] = jnp.where(allowed, scores[0], NEGATIVE)
                    top = jnp.full((1, COLS), 0.1 * NEGATIVE, F32)
                    for s in scores:
                        top = jnp.maximum(top, jnp.max(s, axis=0, keepdims=True))
                    total = jnp.zeros((1, COLS), F32)
                    for j, s in enumerate(scores):
                        prob = jnp.exp2(s - top)
                        total += jnp.sum(prob, axis=0, keepdims=True)
                        prob_ref[other, x, j] = prob.astype(BF)
                    norm = jnp.maximum(top + jnp.log2(total), NEGATIVE)
                    for h in range(HEADS):
                        lanes = slice(h * TOK, (h + 1) * TOK)
                        top_ref[other, x, h : h + 1, :] = top[:, lanes]
                        piece = jnp.broadcast_to(norm[:, lanes], (8, TOK))
                        out_ref[:, from_core, x, h : h + 1, :] = piece.reshape(8, 1, TOK)
                    blocks(prob_ref, prob_hbm, n, other, x, sems).start()

        sources(0)
        sources(1)
        for other in range(2):
            for x in range(4):
                blocks(prob_ref, prob_hbm, n, other, x, sems).wait()

    by_count(place, body)


def raw_scores(
    same_ref, other_ref, kv_ref, prob_hbm, score_hbm, prob_ref, score_ref, in_sems, out_sems
):
    def body(n):
        for x in range(4):
            for other in range(2):
                blocks(prob_hbm, prob_ref, n, other, x, in_sems).start()

        def sources(x, _):
            for other, g_ref in enumerate((same_ref, other_ref)):
                cot = g_ref[x, COLS : 2 * COLS, :]
                tail = g_ref[x, 2 * COLS :, :].astype(F32)
                delta = flat(tail[0:HEADS] + tail[HEADS : 2 * HEADS])
                blocks(prob_hbm, prob_ref, n, other, x, in_sems).wait()
                for j in range(n):
                    dprob = dot(key_block(kv_ref, 1, j), cot, NT)
                    score_ref[other, x, j] = (
                        prob_ref[other, x, j].astype(F32) * (dprob - delta)
                    ).astype(BF)
                blocks(score_ref, score_hbm, n, other, x, out_sems).start()
            return 0

        lax.fori_loop(0, 4, sources, 0)
        for x in range(4):
            for other in range(2):
                blocks(score_ref, score_hbm, n, other, x, out_sems).wait()

    by_count(position(), body)


def over_sources(left_ref, right_ref, j):
    total = None
    for other in range(2):
        for x in range(4):
            part = dot(left_ref[other, x, j], right_ref[other, x], NN)
            total = part if total is None else total + part
    return total


def key_gradients(
    same_ref, other_ref, norm_ref, top_ref, prob_hbm, score_hbm,
    dkv_ref, weight_ref, q_ref, g_ref, prob_ref, score_ref, sems,
):
    place = position()
    core = place[3]
    count = slot_count(place[0])

    def fetch(j, kind):
        far, near = ((score_hbm, score_ref), (prob_hbm, prob_ref))[kind]
        return pltpu.make_async_copy(far.at[:, :, j], near.at[:, :, j], sems.at[j, kind])

    for j in range(SLOTS):

        @pl.when(j < count)
        def _(j=j):
            fetch(j, 0).start()
            fetch(j, 1).start()

    norms = norm_ref[...]
    top = jnp.max(norms, axis=0)
    log_norm = top + jnp.log2(jnp.sum(jnp.exp2(norms - top[None]), axis=0))
    own = jnp.where(core == 0, log_norm[0], log_norm[1])
    far = jnp.where(core == 0, log_norm[1], log_norm[0])
    weight_ref[0] = jnp.exp2(top_ref[0] - own)
    weight_ref[1] = jnp.exp2(top_ref[1] - far)

    def scaled(x, _):
        for other, source_ref in enumerate((same_ref, other_ref)):
            weights = weight_ref[other, x]
            for h in range(HEADS):
                rows = slice(h * TOK, (h + 1) * TOK)
                below = slice(COLS + h * TOK, COLS + (h + 1) * TOK)
                by_row = jnp.broadcast_to(weights[h : h + 1], (TOK, TOK)).T
                q = source_ref[x, rows, :].astype(F32) * (by_row * SCALE)
                q_ref[other, x, rows, :] = q.astype(BF)
                g_ref[other, x, rows, :] = (
                    source_ref[x, below, :].astype(F32) * by_row
                ).astype(BF)
        return 0

    lax.fori_loop(0, 4, scaled, 0)

    def body(n):
        for s in range(SLOTS):
            for kind, left_ref, right_ref in ((0, score_ref, q_ref), (1, prob_ref, g_ref)):
                if s < n:
                    fetch(s, kind).wait()
                    total = over_sources(left_ref, right_ref, s).astype(BF)
                else:
                    total = jnp.zeros((KEYS, HEAD), BF)
                for r in range(GROUP):
                    dkv_ref[2 * r + kind, s * HALF : (s + 1) * HALF, :] = total[
                        r * HALF : (r + 1) * HALF
                    ]

    by_count(place, body)


def query_gradients(
    kv_ref, score_hbm, weight_ref, same_ref, other_ref, turned_ref, score_ref, sems
):

    def body(n):
        for x in range(4):
            for other in (1, 0):
                blocks(score_hbm, score_ref, n, other, x, sems).start()
        for s in range(n):
            turned_ref[s] = key_block(kv_ref, 0, s).astype(F32).T.astype(BF)

        def sources(x, _):
            for other, dq_ref in ((1, other_ref), (0, same_ref)):
                blocks(score_hbm, score_ref, n, other, x, sems).wait()
                dq = dot(turned_ref[0], score_ref[other, x, 0], NN)
                for j in range(1, n):
                    dq += dot(turned_ref[j], score_ref[other, x, j], NN)
                dq_ref[x] = (dq * (flat(weight_ref[other, x]) * SCALE)).astype(BF)
            return 0

        lax.fori_loop(0, 4, sources, 0)

    by_count(position(), body)


def sum_keys(dkv_ref, own_ref, one_ref, two_ref):
    for s, ref in enumerate((own_ref, one_ref, two_ref)):
        for half in range(2):
            total = dkv_ref[half, s * HALF : (s + 1) * HALF, :].astype(F32)
            for r in range(1, GROUP):
                total += dkv_ref[2 * r + half, s * HALF : (s + 1) * HALF, :].astype(F32)
            ref[half * HALF : (half + 1) * HALF, :] = total.astype(ref.dtype)


def sum_cores(same_ref, other_ref, out_ref):
    out_ref[...] = (same_ref[...].astype(F32) + other_ref[...].astype(F32)).astype(BF)


def finish_keys(own_ref, one_ref, two_ref, out_ref):
    out_ref[...] = (
        own_ref[...] + one_ref[...].astype(F32) + two_ref[...].astype(F32)
    ).astype(BF)


def finish_queries(dq_ref, out_ref):
    total = dq_ref[0].astype(F32)
    for x in range(1, 4):
        total += dq_ref[x].astype(F32)
    for h in range(HEADS):
        lanes = slice(h * HEAD, (h + 1) * HEAD)
        out_ref[:, lanes] = total[:, lanes].T.astype(BF)


def local_kernels(same, other, kv, exchange):
    norms, tops, prob = call(
        row_sums,
        "row_sums",
        (
            pltpu.VMEM((8, 2, 4, HEADS, TOK), F32),
            pltpu.VMEM((2, 4, HEADS, TOK), F32),
            pltpu.HBM(FULL, BF),
        ),
        [
            pltpu.VMEM((TOK, TOK), F32),
            pltpu.VMEM((KEYS, TOK), F32),
            pltpu.VMEM(FULL, BF),
            pltpu.SemaphoreType.DMA((2, 4)),
        ],
        near=range(3),
        far_out=(2,),
    )(same, other, kv)
    norms = exchange(norms)
    scores = call(
        raw_scores,
        "raw_scores",
        pltpu.HBM(FULL, BF),
        [
            pltpu.VMEM(FULL, BF),
            pltpu.VMEM(FULL, BF),
            pltpu.SemaphoreType.DMA((2, 4)),
            pltpu.SemaphoreType.DMA((2, 4)),
        ],
        near=range(3),
        far=(3,),
        far_out=(0,),
    )(same, other, kv, prob)
    dkv, weights = call(
        key_gradients,
        "key_gradients",
        (
            pltpu.VMEM((2 * GROUP, SLOTS * HALF, HEAD), BF),
            pltpu.VMEM((2, 4, HEADS, TOK), F32),
        ),
        [
            pltpu.VMEM((2, 4, COLS, HEAD), BF),
            pltpu.VMEM((2, 4, COLS, HEAD), BF),
            pltpu.VMEM(FULL, BF),
            pltpu.VMEM(FULL, BF),
            pltpu.SemaphoreType.DMA((SLOTS, 2)),
        ],
        near=range(4),
        far=(4, 5),
    )(same, other, norms, tops, prob, scores)
    dq_same, dq_other = call(
        query_gradients,
        "query_gradients",
        (pltpu.VMEM((4, HEAD, COLS), BF), pltpu.VMEM((4, HEAD, COLS), BF)),
        [
            pltpu.VMEM((SLOTS, HEAD, KEYS), BF),
            pltpu.VMEM(FULL, BF),
            pltpu.SemaphoreType.DMA((2, 4)),
        ],
        near=(0, 2),
        far=(1,),
    )(kv, scores, weights)
    return dkv, dq_same, dq_other


def per_device(queries, stored_key_value, out_grad, attn_out, segment_ids, loss_mask):
    seg = segment_ids.reshape(1, TOK)
    mask = loss_mask.reshape(1, TOK)
    swap = [(0, 1), (1, 0)]

    two = lax.ppermute(stored_key_value, Z_AXES, FAR)
    one = lax.ppermute(stored_key_value, "zg", [(0, 1), (1, 2)])
    wide = pltpu.VMEM((TOK, HEADS * HEAD), BF)
    line = pltpu.VMEM((1, TOK), jnp.int32)
    packed = call(
        pack_queries,
        "pack_queries",
        pltpu.VMEM((4, Q_ROWS, HEAD), BF),
        [wide, wide, wide, line, line, pltpu.SemaphoreType.DMA((5,))],
        far=range(5),
    )(queries, out_grad, attn_out, seg, mask)
    same = lax.all_to_all(packed, X_AXES, 0, 0, tiled=True)
    other = lax.ppermute(same, "core", swap)
    kv = call(
        pack_keys, "pack_keys", pltpu.VMEM((2 * GROUP, KV_ROWS, HEAD), BF), near=range(4)
    )(
        stored_key_value, two, one, seg
    )
    kv = lax.all_to_all(kv, ("zr", "pair"), 0, 0, tiled=True).reshape(GROUP, 2, KV_ROWS, HEAD)

    dkv, dq_same, dq_other = local_kernels(
        same, other, kv, lambda norms: lax.all_to_all(norms, PLANE, 0, 0, tiled=True)
    )
    dkv = lax.all_to_all(dkv, ("zr", "pair"), 0, 0, tiled=True)
    dq_other = lax.ppermute(dq_other, "core", swap)
    dq = call(sum_cores, "sum_cores", pltpu.VMEM((4, HEAD, COLS), BF), near=(0, 1))(
        dq_same, dq_other
    )
    dkv, dq = lax.optimization_barrier((dkv, dq))
    own, one, two = call(
        sum_keys,
        "sum_keys",
        (
            pltpu.VMEM((TOK, HEAD), F32),
            pltpu.VMEM((TOK, HEAD), BF),
            pltpu.VMEM((TOK, HEAD), BF),
        ),
        near=(0,),
    )(dkv)
    one = lax.ppermute(one, "zg", [(1, 0), (2, 1)])
    two = lax.ppermute(two, Z_AXES, [(b, a) for a, b in FAR])
    dq = lax.all_to_all(dq, X_AXES, 0, 0, tiled=True)
    kv_grad = call(
        finish_keys, "finish_keys", shape((TOK, HEAD), BF), near=range(3), cost=LONG
    )(own, one, two)
    dq, kv_grad = lax.optimization_barrier((dq, kv_grad))
    query_gradient = call(
        finish_queries, "finish_queries", shape((TOK, HEADS * HEAD), BF), near=(0,)
    )(dq)
    return query_gradient, kv_grad


def solution(mesh):
    fine = Mesh(
        mesh.devices.reshape(4, 4, 2, 2, 4, 2), ("zg", "zr", "xh", "core", "tp", "pair")
    )
    rows = ("zg", "zr", "xh", "core")
    wide = P(rows, ("tp", "pair"))
    return jax.shard_map(
        per_device,
        mesh=fine,
        in_specs=(wide, wide, wide, wide, P(rows), P(rows)),
        out_specs=(wide, wide),
        check_vma=False,
    )
```

```python
import functools
import math

import jax
import jax.numpy as jnp
from jax import lax
from jax.experimental import pallas as pl
from jax.experimental.pallas import tpu as pltpu
from jax.sharding import Mesh, PartitionSpec as P

BF = jnp.bfloat16
F32 = jnp.float32
NEGATIVE = -1e30
TOK = 128
HEAD = 128
HEADS = 4
COLS = HEADS * TOK
GROUP = 4
SLOTS = 3
HALF = TOK // 2
KEYS = GROUP * HALF
Q_ROWS = 2 * COLS + 16
KV_ROWS = SLOTS * HALF + 16
FULL = (2, 4, SLOTS, KEYS, COLS)
SCALE = 1.0 / math.sqrt(HEAD)
SCALE2 = SCALE * math.log2(math.e)
LOG_SCALE = math.log2(SCALE)
X_AXES = ("xh", "pair")
Z_AXES = ("zg", "zr")
FAR = [(r, 8 + (r + 2) % 4) for r in range(4)]
PLANE = ("xh", "core", "pair")
NT = (((1,), (1,)), ((), ()))
NN = (((1,), (0,)), ((), ()))
VMEM_LIMIT = 40 * 1024 * 1024
LONG = pl.CostEstimate(flops=40_000_000_000, bytes_accessed=120_000_000, transcendentals=0)


def dot(a, b, dims):
    return lax.dot_general(a, b, dims, preferred_element_type=F32)


def call(kernel, name, out_shape, scratch=(), near=(), far=(), far_out=(), cost=None):
    def bound(*args):
        specs = [
            pl.BlockSpec(memory_space=pltpu.HBM if i in far else pltpu.VMEM)
            for i in range(len(args))
        ]
        outs = out_shape if isinstance(out_shape, tuple) else (out_shape,)
        out_specs = tuple(
            pl.BlockSpec(memory_space=pltpu.HBM if i in far_out else pltpu.VMEM)
            for i in range(len(outs))
        )
        kept = [
            pltpu.with_memory_space_constraint(a, pltpu.VMEM if i in near else pltpu.HBM)
            for i, a in enumerate(args)
        ]
        run = pl.pallas_call(
            kernel,
            out_shape=outs,
            in_specs=specs,
            out_specs=out_specs,
            scratch_shapes=scratch,
            name=name,
            cost_estimate=cost,
            compiler_params=pltpu.CompilerParams(vmem_limit_bytes=VMEM_LIMIT),
        )
        got = run(*kept)
        return got if isinstance(out_shape, tuple) else got[0]

    return bound


def shape(dims, dtype):
    return jax.ShapeDtypeStruct(dims, dtype)


def pack_queries(
    q_hbm, g_hbm, o_hbm, seg_hbm, mask_hbm, kv_hbm,
    out_ref, own_ref,
    q_ref, g_ref, o_ref, seg_ref, mask_ref, kv_ref, sems,
):
    copies = [
        pltpu.make_async_copy(far, ref, sems.at[i])
        for i, (far, ref) in enumerate(
            (
                (q_hbm, q_ref),
                (mask_hbm, mask_ref),
                (seg_hbm, seg_ref),
                (g_hbm, g_ref),
                (o_hbm, o_ref),
                (kv_hbm, kv_ref),
            )
        )
    ]
    for copy in copies:
        copy.start()
    copies[0].wait()
    for h in range(HEADS):
        out_ref[h * TOK : (h + 1) * TOK, :] = q_ref[:, h * HEAD : (h + 1) * HEAD]
    for copy in copies[1:]:
        copy.wait()
    mask = jnp.broadcast_to(mask_ref[...].astype(F32), (TOK, TOK)).T
    rows = []
    for h in range(HEADS):
        lanes = slice(h * HEAD, (h + 1) * HEAD)
        cot = g_ref[:, lanes].astype(F32) * mask
        rows.append(jnp.sum((cot * o_ref[:, lanes].astype(F32)).T, axis=0, keepdims=True))
        out_ref[COLS + h * TOK : COLS + (h + 1) * TOK, :] = cot.astype(BF)
    delta = jnp.concatenate(rows, axis=0)
    high = delta.astype(BF).astype(F32)
    low = delta - high
    seg = seg_ref[...].astype(F32)
    out_ref[2 * COLS :, :] = jnp.concatenate(
        [high, low, seg, jnp.zeros((7, TOK), F32)], axis=0
    ).astype(BF)
    own_ref[:TOK, :] = kv_ref[...]
    own_ref[TOK:, :] = jnp.concatenate([seg, jnp.zeros((15, TOK), F32)], axis=0).astype(BF)


def gather_sources(both_ref, far_ref, near_ref, own_ref, out_ref):
    place = position()
    own = 2 * place[2] + place[4]
    for step, ref in enumerate((own_ref, near_ref, far_ref, both_ref)):
        out_ref[own ^ step] = ref[...]


def pack_keys(own_ref, one_ref, two_ref, out_ref):
    tail = own_ref[TOK:, :]
    for s, ref in enumerate((own_ref, one_ref, two_ref)):
        for half in range(2):
            part = ref[half * HALF : (half + 1) * HALF, :]
            for r in range(GROUP):
                out_ref[2 * r + half, s * HALF : (s + 1) * HALF, :] = part
    for i in range(2 * GROUP):
        out_ref[i, SLOTS * HALF :, :] = tail


def position():
    return (
        lax.axis_index("zg"),
        lax.axis_index("zr"),
        lax.axis_index("xh"),
        lax.axis_index("core"),
        lax.axis_index("pair"),
    )


def slot_count(zg):
    return jnp.where(zg == 3, 1, zg + 1)


def key_block(kv_ref, kind, s):
    first = s * HALF if isinstance(s, int) else pl.multiple_of(s * HALF, HALF)
    return kv_ref[:, kind, pl.ds(first, HALF), :].reshape(KEYS, HEAD)


def key_segments(kv_ref, pair, turn_ref, seg_ref):
    for r in range(GROUP):
        row = kv_ref[r, 0, SLOTS * HALF :, :].astype(F32)[0:1]
        turn_ref[...] = jnp.broadcast_to(row, (TOK, TOK)).T
        seg_ref[r * HALF : (r + 1) * HALF, :] = turn_ref[
            pl.ds(pl.multiple_of(pair * HALF, HALF), HALF), :
        ]


def allowed_pairs(place, query_seg, hx, from_core, seg_ref):
    zg, zr, xh, core, pair = place
    row = lax.broadcasted_iota(jnp.int32, (KEYS, TOK), 0)
    key_pos = (row // HALF) * 512 + row % HALF + ((2 * xh + core) * TOK + pair * HALF)
    lane = lax.broadcasted_iota(jnp.int32, (KEYS, TOK), 1)
    query_pos = lane + (zr * 512 + (2 * hx + from_core) * TOK)
    return (key_pos <= query_pos) & (seg_ref[...] == query_seg)


def tiled(mask):
    return jnp.concatenate([mask] * HEADS, axis=1)


def by_count(place, body):
    count = slot_count(place[0])
    for n in (1, 2, 3):

        @pl.when(count == n)
        def _(n=n):
            body(n)


def flat(rows):
    return jnp.concatenate([rows[h : h + 1] for h in range(HEADS)], axis=1)


def blocks(from_ref, to_ref, n, other, x, sems):
    return pltpu.make_async_copy(
        from_ref.at[other, x, pl.ds(0, n)], to_ref.at[other, x, pl.ds(0, n)], sems.at[other, x]
    )


def row_sums(
    same_ref, other_ref, kv_ref, out_ref, top_ref, prob_hbm, turn_ref, seg_ref, prob_ref, sems
):
    place = position()
    core, pair = place[3:]
    key_segments(kv_ref, pair, turn_ref, seg_ref)

    def body(n):
        def sources(hx):
            for other, q_ref in enumerate((same_ref, other_ref)):
                from_core = (1 - core) if other else core
                segs = q_ref[2 * hx, 2 * COLS :, :].astype(F32)[8:9]
                allowed = tiled(allowed_pairs(place, segs, hx, from_core, seg_ref))
                for p in range(2):
                    x = 2 * hx + p
                    q = q_ref[x, :COLS, :]
                    scores = [dot(key_block(kv_ref, 0, j), q, NT) * SCALE2 for j in range(n)]
                    scores[0] = jnp.where(allowed, scores[0], NEGATIVE)
                    top = jnp.full((1, COLS), 0.1 * NEGATIVE, F32)
                    for s in scores:
                        top = jnp.maximum(top, jnp.max(s, axis=0, keepdims=True))
                    total = jnp.zeros((1, COLS), F32)
                    for j, s in enumerate(scores):
                        prob = jnp.exp2(s - top)
                        total += jnp.sum(prob, axis=0, keepdims=True)
                        prob_ref[other, x, j] = prob.astype(BF)
                    norm = jnp.maximum(top + jnp.log2(total), NEGATIVE)
                    for h in range(HEADS):
                        lanes = slice(h * TOK, (h + 1) * TOK)
                        top_ref[other, x, h : h + 1, :] = top[:, lanes]
                        piece = jnp.broadcast_to(norm[:, lanes], (8, TOK))
                        out_ref[:, from_core, x, h : h + 1, :] = piece.reshape(8, 1, TOK)
                    blocks(prob_ref, prob_hbm, n, other, x, sems).start()

        sources(0)
        sources(1)
        for other in range(2):
            for x in range(4):
                blocks(prob_ref, prob_hbm, n, other, x, sems).wait()

    by_count(place, body)


def raw_scores(
    same_ref, other_ref, kv_ref, prob_hbm, score_hbm, prob_ref, score_ref, in_sems, out_sems
):
    def body(n):
        for x in range(4):
            for other in range(2):
                blocks(prob_hbm, prob_ref, n, other, x, in_sems).start()

        def sources(x, _):
            for other, g_ref in enumerate((same_ref, other_ref)):
                cot = g_ref[x, COLS : 2 * COLS, :]
                tail = g_ref[x, 2 * COLS :, :].astype(F32)
                delta = flat(tail[0:HEADS] + tail[HEADS : 2 * HEADS])
                blocks(prob_hbm, prob_ref, n, other, x, in_sems).wait()
                for j in range(n):
                    dprob = dot(key_block(kv_ref, 1, j), cot, NT)
                    score_ref[other, x, j] = (
                        prob_ref[other, x, j].astype(F32) * (dprob - delta)
                    ).astype(BF)
                blocks(score_ref, score_hbm, n, other, x, out_sems).start()
            return 0

        lax.fori_loop(0, 4, sources, 0)
        for x in range(4):
            for other in range(2):
                blocks(score_ref, score_hbm, n, other, x, out_sems).wait()

    by_count(position(), body)


def over_sources(left_ref, right_ref, j):
    total = None
    for other in range(2):
        for x in range(4):
            part = dot(left_ref[other, x, j], right_ref[other, x], NN)
            total = part if total is None else total + part
    return total


def key_gradients(
    same_ref, other_ref, norm_ref, top_ref, prob_hbm, score_hbm,
    dkv_ref, weight_ref, q_ref, g_ref, prob_ref, score_ref, sems,
):
    place = position()
    core = place[3]
    count = slot_count(place[0])

    def fetch(j, kind):
        far, near = ((score_hbm, score_ref), (prob_hbm, prob_ref))[kind]
        return pltpu.make_async_copy(far.at[:, :, j], near.at[:, :, j], sems.at[j, kind])

    for j in range(SLOTS):

        @pl.when(j < count)
        def _(j=j):
            fetch(j, 0).start()
            fetch(j, 1).start()

    norms = norm_ref[...]
    top = jnp.max(norms, axis=0)
    log_norm = top + jnp.log2(jnp.sum(jnp.exp2(norms - top[None]), axis=0))
    own = jnp.where(core == 0, log_norm[0], log_norm[1])
    far = jnp.where(core == 0, log_norm[1], log_norm[0])
    weight_ref[0] = jnp.exp2(top_ref[0] - own)
    weight_ref[1] = jnp.exp2(top_ref[1] - far)

    for other, source_ref in enumerate((same_ref, other_ref)):
        columns = jnp.concatenate(
            [weight_ref[other].reshape(4 * HEADS, TOK), jnp.zeros((TOK - 4 * HEADS, TOK), F32)],
            axis=0,
        ).T
        for x in range(4):
            for h in range(HEADS):
                rows = slice(h * TOK, (h + 1) * TOK)
                below = slice(COLS + h * TOK, COLS + (h + 1) * TOK)
                i = x * HEADS + h
                by_row = jnp.broadcast_to(columns[:, i : i + 1], (TOK, HEAD))
                q = source_ref[x, rows, :].astype(F32) * (by_row * SCALE)
                q_ref[other, x, rows, :] = q.astype(BF)
                g_ref[other, x, rows, :] = (
                    source_ref[x, below, :].astype(F32) * by_row
                ).astype(BF)

    def body(n):
        for s in range(SLOTS):
            for kind, left_ref, right_ref in ((0, score_ref, q_ref), (1, prob_ref, g_ref)):
                if s < n:
                    fetch(s, kind).wait()
                    total = over_sources(left_ref, right_ref, s).astype(BF)
                else:
                    total = jnp.zeros((KEYS, HEAD), BF)
                for r in range(GROUP):
                    dkv_ref[2 * r + kind, s * HALF : (s + 1) * HALF, :] = total[
                        r * HALF : (r + 1) * HALF
                    ]

    by_count(place, body)


def query_gradients(
    kv_ref, score_hbm, weight_ref, same_ref, other_ref, turned_ref, score_ref, sems
):

    def body(n):
        for x in range(4):
            for other in (1, 0):
                blocks(score_hbm, score_ref, n, other, x, sems).start()
        for s in range(n):
            turned_ref[s] = key_block(kv_ref, 0, s).astype(F32).T.astype(BF)

        def sources(x, _):
            for other, dq_ref in ((1, other_ref), (0, same_ref)):
                blocks(score_hbm, score_ref, n, other, x, sems).wait()
                dq = dot(turned_ref[0], score_ref[other, x, 0], NN)
                for j in range(1, n):
                    dq += dot(turned_ref[j], score_ref[other, x, j], NN)
                dq_ref[x] = (dq * (flat(weight_ref[other, x]) * SCALE)).astype(BF)
            return 0

        lax.fori_loop(0, 4, sources, 0)

    by_count(position(), body)


def sum_keys(dkv_ref, own_ref, one_ref, two_ref):
    for s, ref in enumerate((own_ref, one_ref, two_ref)):
        for half in range(2):
            total = dkv_ref[half, s * HALF : (s + 1) * HALF, :].astype(F32)
            for r in range(1, GROUP):
                total += dkv_ref[2 * r + half, s * HALF : (s + 1) * HALF, :].astype(F32)
            ref[half * HALF : (half + 1) * HALF, :] = total.astype(ref.dtype)


def sum_cores(same_ref, other_ref, out_ref):
    out_ref[...] = (same_ref[...].astype(F32) + other_ref[...].astype(F32)).astype(BF)


def finish_keys(own_ref, two_ref, one_ref, out_ref):
    out_ref[...] = (
        own_ref[...] + one_ref[...].astype(F32) + two_ref[...].astype(F32)
    ).astype(BF)


def finish_queries(dq_ref, out_ref):
    total = dq_ref[0].astype(F32)
    for x in range(1, 4):
        total += dq_ref[x].astype(F32)
    for h in range(HEADS):
        lanes = slice(h * HEAD, (h + 1) * HEAD)
        out_ref[:, lanes] = total[:, lanes].T.astype(BF)


def local_kernels(same, other, kv, exchange):
    norms, tops, prob = call(
        row_sums,
        "row_sums",
        (
            pltpu.VMEM((8, 2, 4, HEADS, TOK), F32),
            pltpu.VMEM((2, 4, HEADS, TOK), F32),
            pltpu.HBM(FULL, BF),
        ),
        [
            pltpu.VMEM((TOK, TOK), F32),
            pltpu.VMEM((KEYS, TOK), F32),
            pltpu.VMEM(FULL, BF),
            pltpu.SemaphoreType.DMA((2, 4)),
        ],
        near=range(3),
        far_out=(2,),
    )(same, other, kv)
    norms = exchange(norms)
    scores = call(
        raw_scores,
        "raw_scores",
        pltpu.HBM(FULL, BF),
        [
            pltpu.VMEM(FULL, BF),
            pltpu.VMEM(FULL, BF),
            pltpu.SemaphoreType.DMA((2, 4)),
            pltpu.SemaphoreType.DMA((2, 4)),
        ],
        near=range(3),
        far=(3,),
        far_out=(0,),
    )(same, other, kv, prob)
    dkv, weights = call(
        key_gradients,
        "key_gradients",
        (
            pltpu.VMEM((2 * GROUP, SLOTS * HALF, HEAD), BF),
            pltpu.VMEM((2, 4, HEADS, TOK), F32),
        ),
        [
            pltpu.VMEM((2, 4, COLS, HEAD), BF),
            pltpu.VMEM((2, 4, COLS, HEAD), BF),
            pltpu.VMEM(FULL, BF),
            pltpu.VMEM(FULL, BF),
            pltpu.SemaphoreType.DMA((SLOTS, 2)),
        ],
        near=range(4),
        far=(4, 5),
    )(same, other, norms, tops, prob, scores)
    dq_same, dq_other = call(
        query_gradients,
        "query_gradients",
        (pltpu.VMEM((4, HEAD, COLS), BF), pltpu.VMEM((4, HEAD, COLS), BF)),
        [
            pltpu.VMEM((SLOTS, HEAD, KEYS), BF),
            pltpu.VMEM(FULL, BF),
            pltpu.SemaphoreType.DMA((2, 4)),
        ],
        near=(0, 2),
        far=(1,),
    )(kv, scores, weights)
    return dkv, dq_same, dq_other


def per_device(queries, stored_key_value, out_grad, attn_out, segment_ids, loss_mask):
    seg = segment_ids.reshape(1, TOK)
    mask = loss_mask.reshape(1, TOK)
    swap = [(0, 1), (1, 0)]

    two = lax.ppermute(stored_key_value, Z_AXES, FAR)
    one = lax.ppermute(stored_key_value, "zg", [(0, 1), (1, 2)])
    wide = pltpu.VMEM((TOK, HEADS * HEAD), BF)
    line = pltpu.VMEM((1, TOK), jnp.int32)
    packed, own = call(
        pack_queries,
        "pack_queries",
        (pltpu.VMEM((Q_ROWS, HEAD), BF), pltpu.VMEM((TOK + 16, HEAD), BF)),
        [wide, wide, wide, line, line, pltpu.VMEM((TOK, HEAD), BF), pltpu.SemaphoreType.DMA((6,))],
        far=range(6),
    )(queries, out_grad, attn_out, seg, mask, stored_key_value)
    near = lax.ppermute(packed, "pair", swap)
    far = lax.ppermute(packed, "xh", swap)
    both = lax.ppermute(packed, X_AXES, [(i, 3 - i) for i in range(4)])
    same = call(
        gather_sources, "gather_sources", pltpu.VMEM((4, Q_ROWS, HEAD), BF), near=range(4), cost=LONG
    )(both, far, near, packed)
    other = lax.ppermute(same, "core", swap)
    kv = call(
        pack_keys, "pack_keys", pltpu.VMEM((2 * GROUP, KV_ROWS, HEAD), BF), near=range(3), cost=LONG
    )(
        own, one, two
    )
    kv = lax.all_to_all(kv, ("zr", "pair"), 0, 0, tiled=True).reshape(GROUP, 2, KV_ROWS, HEAD)

    dkv, dq_same, dq_other = local_kernels(
        same, other, kv, lambda norms: lax.all_to_all(norms, PLANE, 0, 0, tiled=True)
    )
    dkv = lax.all_to_all(dkv, ("zr", "pair"), 0, 0, tiled=True)
    dq_other = lax.ppermute(dq_other, "core", swap)
    dq = call(sum_cores, "sum_cores", pltpu.VMEM((4, HEAD, COLS), BF), near=(0, 1))(
        dq_same, dq_other
    )
    dkv, dq = lax.optimization_barrier((dkv, dq))
    own, one, two = call(
        sum_keys,
        "sum_keys",
        (
            pltpu.VMEM((TOK, HEAD), F32),
            pltpu.VMEM((TOK, HEAD), BF),
            pltpu.VMEM((TOK, HEAD), BF),
        ),
        near=(0,),
    )(dkv)
    two = lax.ppermute(two, Z_AXES, [(b, a) for a, b in FAR])
    one = lax.ppermute(one, "zg", [(1, 0), (2, 1)])
    dq = lax.all_to_all(dq, X_AXES, 0, 0, tiled=True)
    kv_grad = call(
        finish_keys, "finish_keys", shape((TOK, HEAD), BF), near=range(3), cost=LONG
    )(own, two, one)
    dq, kv_grad = lax.optimization_barrier((dq, kv_grad))
    query_gradient = call(
        finish_queries, "finish_queries", shape((TOK, HEADS * HEAD), BF), near=(0,)
    )(dq)
    return query_gradient, kv_grad


def solution(mesh):
    fine = Mesh(
        mesh.devices.reshape(4, 4, 2, 2, 4, 2), ("zg", "zr", "xh", "core", "tp", "pair")
    )
    rows = ("zg", "zr", "xh", "core")
    wide = P(rows, ("tp", "pair"))
    return jax.shard_map(
        per_device,
        mesh=fine,
        in_specs=(wide, wide, wide, wide, P(rows), P(rows)),
        out_specs=(wide, wide),
        check_vma=False,
    )
```

```python
import functools
import math

import jax
import jax.numpy as jnp
from jax import lax
from jax.experimental import pallas as pl
from jax.experimental.pallas import tpu as pltpu
from jax.sharding import Mesh, PartitionSpec as P

BF = jnp.bfloat16
F32 = jnp.float32
NEGATIVE = -1e30
TOK = 128
HEAD = 128
HEADS = 4
COLS = HEADS * TOK
GROUP = 4
SLOTS = 3
HALF = TOK // 2
KEYS = GROUP * HALF
Q_ROWS = 2 * COLS + 16
KV_ROWS = SLOTS * HALF + 16
FULL = (2, 4, SLOTS, KEYS, COLS)
SCALE = 1.0 / math.sqrt(HEAD)
SCALE2 = SCALE * math.log2(math.e)
LOG_SCALE = math.log2(SCALE)
X_AXES = ("xh", "pair")
Z_AXES = ("zg", "zr")
FAR = [(r, 8 + (r + 2) % 4) for r in range(4)]
PLANE = ("xh", "core", "pair")
NT = (((1,), (1,)), ((), ()))
NN = (((1,), (0,)), ((), ()))
VMEM_LIMIT = 40 * 1024 * 1024
LONG = pl.CostEstimate(flops=40_000_000_000, bytes_accessed=120_000_000, transcendentals=0)


def dot(a, b, dims):
    return lax.dot_general(a, b, dims, preferred_element_type=F32)


def call(kernel, name, out_shape, scratch=(), near=(), far=(), far_out=(), cost=None):
    def bound(*args):
        specs = [
            pl.BlockSpec(memory_space=pltpu.HBM if i in far else pltpu.VMEM)
            for i in range(len(args))
        ]
        outs = out_shape if isinstance(out_shape, tuple) else (out_shape,)
        out_specs = tuple(
            pl.BlockSpec(memory_space=pltpu.HBM if i in far_out else pltpu.VMEM)
            for i in range(len(outs))
        )
        kept = [
            pltpu.with_memory_space_constraint(a, pltpu.VMEM if i in near else pltpu.HBM)
            for i, a in enumerate(args)
        ]
        run = pl.pallas_call(
            kernel,
            out_shape=outs,
            in_specs=specs,
            out_specs=out_specs,
            scratch_shapes=scratch,
            name=name,
            cost_estimate=cost,
            compiler_params=pltpu.CompilerParams(vmem_limit_bytes=VMEM_LIMIT),
        )
        got = run(*kept)
        return got if isinstance(out_shape, tuple) else got[0]

    return bound


def shape(dims, dtype):
    return jax.ShapeDtypeStruct(dims, dtype)


def pack_queries(
    q_hbm, g_hbm, o_hbm, seg_hbm, mask_hbm, kv_hbm,
    out_ref, own_ref,
    q_ref, g_ref, o_ref, seg_ref, mask_ref, kv_ref, sems,
):
    copies = [
        pltpu.make_async_copy(far, ref, sems.at[i])
        for i, (far, ref) in enumerate(
            (
                (q_hbm, q_ref),
                (mask_hbm, mask_ref),
                (seg_hbm, seg_ref),
                (g_hbm, g_ref),
                (o_hbm, o_ref),
                (kv_hbm, kv_ref),
            )
        )
    ]
    for copy in copies:
        copy.start()
    copies[0].wait()
    for h in range(HEADS):
        out_ref[h * TOK : (h + 1) * TOK, :] = q_ref[:, h * HEAD : (h + 1) * HEAD]
    for copy in copies[1:]:
        copy.wait()
    mask = jnp.broadcast_to(mask_ref[...].astype(F32), (TOK, TOK)).T
    rows = []
    for h in range(HEADS):
        lanes = slice(h * HEAD, (h + 1) * HEAD)
        cot = g_ref[:, lanes].astype(F32) * mask
        rows.append(jnp.sum((cot * o_ref[:, lanes].astype(F32)).T, axis=0, keepdims=True))
        out_ref[COLS + h * TOK : COLS + (h + 1) * TOK, :] = cot.astype(BF)
    delta = jnp.concatenate(rows, axis=0)
    high = delta.astype(BF).astype(F32)
    low = delta - high
    seg = seg_ref[...].astype(F32)
    out_ref[2 * COLS :, :] = jnp.concatenate(
        [high, low, seg, jnp.zeros((7, TOK), F32)], axis=0
    ).astype(BF)
    own_ref[:TOK, :] = kv_ref[...]
    own_ref[TOK:, :] = jnp.concatenate([seg, jnp.zeros((15, TOK), F32)], axis=0).astype(BF)


def gather_sources(both_ref, far_ref, near_ref, own_ref, out_ref):
    place = position()
    own = 2 * place[2] + place[4]
    for step, ref in enumerate((own_ref, near_ref, far_ref, both_ref)):
        out_ref[own ^ step] = ref[...]


def pack_keys(own_ref, one_ref, two_ref, out_ref):
    tail = own_ref[TOK:, :]
    for s, ref in enumerate((own_ref, one_ref, two_ref)):
        for half in range(2):
            part = ref[half * HALF : (half + 1) * HALF, :]
            for r in range(GROUP):
                out_ref[2 * r + half, s * HALF : (s + 1) * HALF, :] = part
    for i in range(2 * GROUP):
        out_ref[i, SLOTS * HALF :, :] = tail


def position():
    return (
        lax.axis_index("zg"),
        lax.axis_index("zr"),
        lax.axis_index("xh"),
        lax.axis_index("core"),
        lax.axis_index("pair"),
    )


def slot_count(zg):
    return jnp.where(zg == 3, 1, zg + 1)


def key_block(kv_ref, kind, s):
    first = s * HALF if isinstance(s, int) else pl.multiple_of(s * HALF, HALF)
    return kv_ref[:, kind, pl.ds(first, HALF), :].reshape(KEYS, HEAD)


def key_segments(kv_ref, pair, turn_ref, seg_ref):
    for r in range(GROUP):
        row = kv_ref[r, 0, SLOTS * HALF :, :].astype(F32)[0:1]
        turn_ref[...] = jnp.broadcast_to(row, (TOK, TOK)).T
        seg_ref[r * HALF : (r + 1) * HALF, :] = turn_ref[
            pl.ds(pl.multiple_of(pair * HALF, HALF), HALF), :
        ]


def allowed_pairs(place, query_seg, hx, from_core, seg_ref):
    zg, zr, xh, core, pair = place
    row = lax.broadcasted_iota(jnp.int32, (KEYS, TOK), 0)
    key_pos = (row // HALF) * 512 + row % HALF + ((2 * xh + core) * TOK + pair * HALF)
    lane = lax.broadcasted_iota(jnp.int32, (KEYS, TOK), 1)
    query_pos = lane + (zr * 512 + (2 * hx + from_core) * TOK)
    return (key_pos <= query_pos) & (seg_ref[...] == query_seg)


def tiled(mask):
    return jnp.concatenate([mask] * HEADS, axis=1)


def by_count(place, body):
    count = slot_count(place[0])
    for n in (1, 2, 3):

        @pl.when(count == n)
        def _(n=n):
            body(n)


def flat(rows):
    return jnp.concatenate([rows[h : h + 1] for h in range(HEADS)], axis=1)


def blocks(from_ref, to_ref, n, other, x, sems):
    return pltpu.make_async_copy(
        from_ref.at[other, x, pl.ds(0, n)], to_ref.at[other, x, pl.ds(0, n)], sems.at[other, x]
    )


def row_sums(
    same_ref, other_ref, kv_ref, out_ref, turn_ref, seg_ref
):
    place = position()
    core, pair = place[3:]
    key_segments(kv_ref, pair, turn_ref, seg_ref)

    def body(n):
        def sources(hx):
            for other, q_ref in enumerate((same_ref, other_ref)):
                from_core = (1 - core) if other else core
                segs = q_ref[2 * hx, 2 * COLS :, :].astype(F32)[8:9]
                allowed = tiled(allowed_pairs(place, segs, hx, from_core, seg_ref))
                for p in range(2):
                    x = 2 * hx + p
                    q = q_ref[x, :COLS, :]
                    scores = [dot(key_block(kv_ref, 0, j), q, NT) * SCALE2 for j in range(n)]
                    scores[0] = jnp.where(allowed, scores[0], NEGATIVE)
                    top = jnp.full((1, COLS), 0.1 * NEGATIVE, F32)
                    for s in scores:
                        top = jnp.maximum(top, jnp.max(s, axis=0, keepdims=True))
                    total = jnp.zeros((1, COLS), F32)
                    for s in scores:
                        total += jnp.sum(jnp.exp2(s - top), axis=0, keepdims=True)
                    norm = jnp.maximum(top + jnp.log2(total), NEGATIVE)
                    for h in range(HEADS):
                        lanes = slice(h * TOK, (h + 1) * TOK)
                        piece = jnp.broadcast_to(norm[:, lanes], (8, TOK))
                        out_ref[:, from_core, x, h : h + 1, :] = piece.reshape(8, 1, TOK)

        sources(0)
        sources(1)

    by_count(place, body)


def key_gradients(
    same_ref, other_ref, kv_ref, norm_ref,
    dkv_ref, score_hbm,
    turn_ref, seg_ref, log_ref, prob_ref, score_ref, sems,
):
    place = position()
    core, pair = place[3:]
    key_segments(kv_ref, pair, turn_ref, seg_ref)
    norms = norm_ref[...]
    top = jnp.max(norms, axis=0)
    log_ref[...] = top + jnp.log2(jnp.sum(jnp.exp2(norms - top[None]), axis=0)) - LOG_SCALE

    def over_sources(left_ref, first, j):
        total = None
        for other, right_ref in enumerate((same_ref, other_ref)):
            for x in range(4):
                part = dot(left_ref[other, x, j], right_ref[x, first : first + COLS, :], NN)
                total = part if total is None else total + part
        return total

    def body(n):
        def sources(hx, _):
            for other, q_ref in enumerate((same_ref, other_ref)):
                from_core = (1 - core) if other else core
                segs = q_ref[2 * hx, 2 * COLS :, :].astype(F32)[8:9]
                allowed = tiled(allowed_pairs(place, segs, hx, from_core, seg_ref))
                for p in range(2):
                    x = 2 * hx + p
                    q = q_ref[x, :COLS, :]
                    cot = q_ref[x, COLS : 2 * COLS, :]
                    tail = q_ref[x, 2 * COLS :, :].astype(F32)
                    delta = flat(tail[0:HEADS] + tail[HEADS : 2 * HEADS])
                    norm = flat(log_ref[from_core, x])
                    for j in range(n):
                        s = dot(key_block(kv_ref, 0, j), q, NT)
                        prob = jnp.exp2(s * SCALE2 - norm)
                        if j == 0:
                            prob = jnp.where(allowed, prob, 0.0)
                        dprob = dot(key_block(kv_ref, 1, j), cot, NT)
                        prob_ref[other, x, j] = prob.astype(BF)
                        score_ref[other, x, j] = (prob * (dprob - delta)).astype(BF)
                    blocks(score_ref, score_hbm, n, other, x, sems).start()
            return 0

        lax.fori_loop(0, 2, sources, 0)
        for s in range(SLOTS):
            for kind, left_ref, scale in ((0, score_ref, 1.0), (1, prob_ref, 1.0 / SCALE)):
                if s < n:
                    total = (over_sources(left_ref, kind * COLS, s) * scale).astype(BF)
                else:
                    total = jnp.zeros((KEYS, HEAD), BF)
                for r in range(GROUP):
                    dkv_ref[2 * r + kind, s * HALF : (s + 1) * HALF, :] = total[
                        r * HALF : (r + 1) * HALF
                    ]
        for other in range(2):
            for x in range(4):
                blocks(score_ref, score_hbm, n, other, x, sems).wait()

    by_count(place, body)


def query_gradients(
    kv_ref, score_hbm, same_ref, other_ref, turned_ref, score_ref, sems
):

    def body(n):
        for x in range(4):
            for other in (1, 0):
                blocks(score_hbm, score_ref, n, other, x, sems).start()
        for s in range(n):
            turned_ref[s] = key_block(kv_ref, 0, s).astype(F32).T.astype(BF)

        def sources(x, _):
            for other, dq_ref in ((1, other_ref), (0, same_ref)):
                blocks(score_hbm, score_ref, n, other, x, sems).wait()
                dq = dot(turned_ref[0], score_ref[other, x, 0], NN)
                for j in range(1, n):
                    dq += dot(turned_ref[j], score_ref[other, x, j], NN)
                dq_ref[x] = dq.astype(BF)
            return 0

        lax.fori_loop(0, 4, sources, 0)

    by_count(position(), body)


def sum_keys(dkv_ref, own_ref, one_ref, two_ref):
    for s, ref in enumerate((own_ref, one_ref, two_ref)):
        for half in range(2):
            total = dkv_ref[half, s * HALF : (s + 1) * HALF, :].astype(F32)
            for r in range(1, GROUP):
                total += dkv_ref[2 * r + half, s * HALF : (s + 1) * HALF, :].astype(F32)
            ref[half * HALF : (half + 1) * HALF, :] = total.astype(ref.dtype)


def sum_cores(same_ref, other_ref, out_ref):
    out_ref[...] = (same_ref[...].astype(F32) + other_ref[...].astype(F32)).astype(BF)


def finish_keys(own_ref, two_ref, one_ref, out_ref):
    out_ref[...] = (
        own_ref[...] + one_ref[...].astype(F32) + two_ref[...].astype(F32)
    ).astype(BF)


def finish_queries(dq_ref, out_ref):
    total = dq_ref[0].astype(F32)
    for x in range(1, 4):
        total += dq_ref[x].astype(F32)
    for h in range(HEADS):
        lanes = slice(h * HEAD, (h + 1) * HEAD)
        out_ref[:, lanes] = total[:, lanes].T.astype(BF)


def local_kernels(same, other, kv, exchange):
    segs = [pltpu.VMEM((TOK, TOK), F32), pltpu.VMEM((KEYS, TOK), F32)]
    norms = call(
        row_sums, "row_sums", pltpu.VMEM((8, 2, 4, HEADS, TOK), F32), segs, near=range(3)
    )(same, other, kv)
    norms = exchange(norms)
    dkv, scores = call(
        key_gradients,
        "key_gradients",
        (pltpu.VMEM((2 * GROUP, SLOTS * HALF, HEAD), BF), pltpu.HBM(FULL, BF)),
        segs
        + [
            pltpu.VMEM((2, 4, HEADS, TOK), F32),
            pltpu.VMEM(FULL, BF),
            pltpu.VMEM(FULL, BF),
            pltpu.SemaphoreType.DMA((2, 4)),
        ],
        near=range(4),
        far_out=(1,),
    )(same, other, kv, norms)
    dq_same, dq_other = call(
        query_gradients,
        "query_gradients",
        (pltpu.VMEM((4, HEAD, COLS), BF), pltpu.VMEM((4, HEAD, COLS), BF)),
        [
            pltpu.VMEM((SLOTS, HEAD, KEYS), BF),
            pltpu.VMEM(FULL, BF),
            pltpu.SemaphoreType.DMA((2, 4)),
        ],
        near=(0,),
        far=(1,),
    )(kv, scores)
    return dkv, dq_same, dq_other


def per_device(queries, stored_key_value, out_grad, attn_out, segment_ids, loss_mask):
    seg = segment_ids.reshape(1, TOK)
    mask = loss_mask.reshape(1, TOK)
    swap = [(0, 1), (1, 0)]

    two = lax.ppermute(stored_key_value, Z_AXES, FAR)
    one = lax.ppermute(stored_key_value, "zg", [(0, 1), (1, 2)])
    wide = pltpu.VMEM((TOK, HEADS * HEAD), BF)
    line = pltpu.VMEM((1, TOK), jnp.int32)
    packed, own = call(
        pack_queries,
        "pack_queries",
        (pltpu.VMEM((Q_ROWS, HEAD), BF), pltpu.VMEM((TOK + 16, HEAD), BF)),
        [wide, wide, wide, line, line, pltpu.VMEM((TOK, HEAD), BF), pltpu.SemaphoreType.DMA((6,))],
        far=range(6),
    )(queries, out_grad, attn_out, seg, mask, stored_key_value)
    near = lax.ppermute(packed, "pair", swap)
    far = lax.ppermute(packed, "xh", swap)
    both = lax.ppermute(packed, X_AXES, [(i, 3 - i) for i in range(4)])
    same = call(
        gather_sources, "gather_sources", pltpu.VMEM((4, Q_ROWS, HEAD), BF), near=range(4), cost=LONG
    )(both, far, near, packed)
    other = lax.ppermute(same, "core", swap)
    kv = call(
        pack_keys, "pack_keys", pltpu.VMEM((2 * GROUP, KV_ROWS, HEAD), BF), near=range(3), cost=LONG
    )(
        own, one, two
    )
    kv = lax.all_to_all(kv, ("zr", "pair"), 0, 0, tiled=True).reshape(GROUP, 2, KV_ROWS, HEAD)

    dkv, dq_same, dq_other = local_kernels(
        same, other, kv, lambda norms: lax.all_to_all(norms, PLANE, 0, 0, tiled=True)
    )
    dkv = lax.all_to_all(dkv, ("zr", "pair"), 0, 0, tiled=True)
    dq_other = lax.ppermute(dq_other, "core", swap)
    dq = call(sum_cores, "sum_cores", pltpu.VMEM((4, HEAD, COLS), BF), near=(0, 1))(
        dq_same, dq_other
    )
    dkv, dq = lax.optimization_barrier((dkv, dq))
    own, one, two = call(
        sum_keys,
        "sum_keys",
        (
            pltpu.VMEM((TOK, HEAD), F32),
            pltpu.VMEM((TOK, HEAD), BF),
            pltpu.VMEM((TOK, HEAD), BF),
        ),
        near=(0,),
    )(dkv)
    two = lax.ppermute(two, Z_AXES, [(b, a) for a, b in FAR])
    one = lax.ppermute(one, "zg", [(1, 0), (2, 1)])
    dq = lax.all_to_all(dq, X_AXES, 0, 0, tiled=True)
    kv_grad = call(
        finish_keys, "finish_keys", shape((TOK, HEAD), BF), near=range(3), cost=LONG
    )(own, two, one)
    dq, kv_grad = lax.optimization_barrier((dq, kv_grad))
    query_gradient = call(
        finish_queries, "finish_queries", shape((TOK, HEADS * HEAD), BF), near=(0,)
    )(dq)
    return query_gradient, kv_grad


def solution(mesh):
    fine = Mesh(
        mesh.devices.reshape(4, 4, 2, 2, 4, 2), ("zg", "zr", "xh", "core", "tp", "pair")
    )
    rows = ("zg", "zr", "xh", "core")
    wide = P(rows, ("tp", "pair"))
    return jax.shard_map(
        per_device,
        mesh=fine,
        in_specs=(wide, wide, wide, wide, P(rows), P(rows)),
        out_specs=(wide, wide),
        check_vma=False,
    )
```

```python
import functools
import math

import jax
import jax.numpy as jnp
from jax import lax
from jax.experimental import pallas as pl
from jax.experimental.pallas import tpu as pltpu
from jax.sharding import Mesh, PartitionSpec as P

BF = jnp.bfloat16
F32 = jnp.float32
NEGATIVE = -1e30
TOK = 128
HEAD = 128
HEADS = 4
COLS = HEADS * TOK
GROUP = 4
SLOTS = 3
HALF = TOK // 2
KEYS = GROUP * HALF
Q_ROWS = 2 * COLS + 16
KV_ROWS = SLOTS * HALF
FULL = (2, 4, SLOTS, KEYS, COLS)
SCALE = 1.0 / math.sqrt(HEAD)
SCALE2 = SCALE * math.log2(math.e)
LOG_SCALE = math.log2(SCALE)
X_AXES = ("xh", "pair")
Z_AXES = ("zg", "zr")
FAR = [(r, 8 + (r + 2) % 4) for r in range(4)]
PLANE = ("xh", "core", "pair")
NT = (((1,), (1,)), ((), ()))
NN = (((1,), (0,)), ((), ()))
VMEM_LIMIT = 40 * 1024 * 1024
LONG = pl.CostEstimate(flops=40_000_000_000, bytes_accessed=120_000_000, transcendentals=0)


def dot(a, b, dims):
    return lax.dot_general(a, b, dims, preferred_element_type=F32)


def call(kernel, name, out_shape, scratch=(), near=(), far=(), far_out=(), cost=None):
    def bound(*args):
        specs = [
            pl.BlockSpec(memory_space=pltpu.HBM if i in far else pltpu.VMEM)
            for i in range(len(args))
        ]
        outs = out_shape if isinstance(out_shape, tuple) else (out_shape,)
        out_specs = tuple(
            pl.BlockSpec(memory_space=pltpu.HBM if i in far_out else pltpu.VMEM)
            for i in range(len(outs))
        )
        kept = [
            pltpu.with_memory_space_constraint(a, pltpu.VMEM if i in near else pltpu.HBM)
            for i, a in enumerate(args)
        ]
        run = pl.pallas_call(
            kernel,
            out_shape=outs,
            in_specs=specs,
            out_specs=out_specs,
            scratch_shapes=scratch,
            name=name,
            cost_estimate=cost,
            compiler_params=pltpu.CompilerParams(vmem_limit_bytes=VMEM_LIMIT),
        )
        got = run(*kept)
        return got if isinstance(out_shape, tuple) else got[0]

    return bound


def shape(dims, dtype):
    return jax.ShapeDtypeStruct(dims, dtype)


def pack_queries(
    q_hbm, g_hbm, o_hbm, seg_hbm, mask_hbm, kv_hbm,
    out_ref, own_ref,
    q_ref, g_ref, o_ref, seg_ref, mask_ref, kv_ref, sems,
):
    copies = [
        pltpu.make_async_copy(far, ref, sems.at[i])
        for i, (far, ref) in enumerate(
            (
                (q_hbm, q_ref),
                (mask_hbm, mask_ref),
                (seg_hbm, seg_ref),
                (g_hbm, g_ref),
                (o_hbm, o_ref),
                (kv_hbm, kv_ref),
            )
        )
    ]
    for copy in copies:
        copy.start()
    copies[0].wait()
    for h in range(HEADS):
        out_ref[h * TOK : (h + 1) * TOK, :] = q_ref[:, h * HEAD : (h + 1) * HEAD]
    for copy in copies[1:]:
        copy.wait()
    mask = jnp.broadcast_to(mask_ref[...].astype(F32), (TOK, TOK)).T
    rows = []
    for h in range(HEADS):
        lanes = slice(h * HEAD, (h + 1) * HEAD)
        cot = g_ref[:, lanes].astype(F32) * mask
        rows.append(jnp.sum((cot * o_ref[:, lanes].astype(F32)).T, axis=0, keepdims=True))
        out_ref[COLS + h * TOK : COLS + (h + 1) * TOK, :] = cot.astype(BF)
    delta = jnp.concatenate(rows, axis=0)
    high = delta.astype(BF).astype(F32)
    low = delta - high
    seg = seg_ref[...].astype(F32)
    out_ref[2 * COLS :, :] = jnp.concatenate(
        [high, low, seg, jnp.zeros((7, TOK), F32)], axis=0
    ).astype(BF)
    own_ref[:TOK, :] = kv_ref[...]
    own_ref[TOK:, :] = jnp.concatenate([seg, jnp.zeros((15, TOK), F32)], axis=0).astype(BF)


def gather_sources(both_ref, far_ref, near_ref, own_ref, out_ref):
    place = position()
    own = 2 * place[2] + place[4]
    for step, ref in enumerate((own_ref, near_ref, far_ref, both_ref)):
        out_ref[own ^ step] = ref[...]


def pack_keys(own_ref, one_ref, two_ref, out_ref):
    tail = own_ref[TOK:, :]
    for s, ref in enumerate((own_ref, one_ref, two_ref)):
        for half in range(2):
            part = ref[half * HALF : (half + 1) * HALF, :]
            for r in range(GROUP):
                out_ref[2 * r + half, s * HALF : (s + 1) * HALF, :] = part

    @pl.when(lax.axis_index("zg") == 3)
    def _():
        for i in range(2 * GROUP):
            out_ref[i, HALF : HALF + 16, :] = tail


def position():
    return (
        lax.axis_index("zg"),
        lax.axis_index("zr"),
        lax.axis_index("xh"),
        lax.axis_index("core"),
        lax.axis_index("pair"),
    )


def slot_count(zg):
    return jnp.where(zg == 3, 1, zg + 1)


def key_block(kv_ref, kind, s):
    first = s * HALF if isinstance(s, int) else pl.multiple_of(s * HALF, HALF)
    return kv_ref[:, kind, pl.ds(first, HALF), :].reshape(KEYS, HEAD)


def key_segments(kv_ref, pair, turn_ref, seg_ref):
    for r in range(GROUP):
        row = kv_ref[r, 0, HALF : HALF + 16, :].astype(F32)[0:1]
        turn_ref[...] = jnp.broadcast_to(row, (TOK, TOK)).T
        seg_ref[r * HALF : (r + 1) * HALF, :] = turn_ref[
            pl.ds(pl.multiple_of(pair * HALF, HALF), HALF), :
        ]


def allowed_pairs(place, query_seg, hx, from_core, seg_ref):
    zg, zr, xh, core, pair = place
    row = lax.broadcasted_iota(jnp.int32, (KEYS, TOK), 0)
    key_pos = (row // HALF) * 512 + row % HALF + ((2 * xh + core) * TOK + pair * HALF)
    lane = lax.broadcasted_iota(jnp.int32, (KEYS, TOK), 1)
    query_pos = lane + (zr * 512 + (2 * hx + from_core) * TOK)
    one_document = jnp.broadcast_to(zg, (KEYS, TOK)) < 3
    return (key_pos <= query_pos) & ((seg_ref[...] == query_seg) | one_document)


def tiled(mask):
    return jnp.concatenate([mask] * HEADS, axis=1)


def by_count(place, body):
    count = slot_count(place[0])
    for n in (1, 2, 3):

        @pl.when(count == n)
        def _(n=n):
            body(n)


def flat(rows):
    return jnp.concatenate([rows[h : h + 1] for h in range(HEADS)], axis=1)


def blocks(from_ref, to_ref, n, other, x, sems):
    return pltpu.make_async_copy(
        from_ref.at[other, x, pl.ds(0, n)], to_ref.at[other, x, pl.ds(0, n)], sems.at[other, x]
    )


def row_sums(
    same_ref, other_ref, kv_ref, out_ref, turn_ref, seg_ref
):
    place = position()
    core, pair = place[3:]
    key_segments(kv_ref, pair, turn_ref, seg_ref)

    def body(n):
        def sources(hx):
            for other, q_ref in enumerate((same_ref, other_ref)):
                from_core = (1 - core) if other else core
                segs = q_ref[2 * hx, 2 * COLS :, :].astype(F32)[8:9]
                allowed = tiled(allowed_pairs(place, segs, hx, from_core, seg_ref))
                for p in range(2):
                    x = 2 * hx + p
                    q = q_ref[x, :COLS, :]
                    scores = [dot(key_block(kv_ref, 0, j), q, NT) * SCALE2 for j in range(n)]
                    scores[0] = jnp.where(allowed, scores[0], NEGATIVE)
                    top = jnp.full((1, COLS), 0.1 * NEGATIVE, F32)
                    for s in scores:
                        top = jnp.maximum(top, jnp.max(s, axis=0, keepdims=True))
                    total = jnp.zeros((1, COLS), F32)
                    for s in scores:
                        total += jnp.sum(jnp.exp2(s - top), axis=0, keepdims=True)
                    norm = jnp.maximum(top + jnp.log2(total), NEGATIVE)
                    for h in range(HEADS):
                        lanes = slice(h * TOK, (h + 1) * TOK)
                        piece = jnp.broadcast_to(norm[:, lanes], (8, TOK))
                        out_ref[:, from_core, x, h : h + 1, :] = piece.reshape(8, 1, TOK)

        sources(0)
        sources(1)

    by_count(place, body)


def key_gradients(
    same_ref, other_ref, kv_ref, norm_ref,
    dkv_ref, score_hbm,
    turn_ref, seg_ref, log_ref, prob_ref, score_ref, sems,
):
    place = position()
    core, pair = place[3:]
    key_segments(kv_ref, pair, turn_ref, seg_ref)
    norms = norm_ref[...]
    top = jnp.max(norms, axis=0)
    log_ref[...] = top + jnp.log2(jnp.sum(jnp.exp2(norms - top[None]), axis=0)) - LOG_SCALE

    def over_sources(left_ref, first, j):
        total = None
        for other, right_ref in enumerate((same_ref, other_ref)):
            for x in range(4):
                part = dot(left_ref[other, x, j], right_ref[x, first : first + COLS, :], NN)
                total = part if total is None else total + part
        return total

    def body(n):
        def sources(hx, _):
            for other, q_ref in enumerate((same_ref, other_ref)):
                from_core = (1 - core) if other else core
                segs = q_ref[2 * hx, 2 * COLS :, :].astype(F32)[8:9]
                allowed = tiled(allowed_pairs(place, segs, hx, from_core, seg_ref))
                for p in range(2):
                    x = 2 * hx + p
                    q = q_ref[x, :COLS, :]
                    cot = q_ref[x, COLS : 2 * COLS, :]
                    tail = q_ref[x, 2 * COLS :, :].astype(F32)
                    delta = flat(tail[0:HEADS] + tail[HEADS : 2 * HEADS])
                    norm = flat(log_ref[from_core, x])
                    for j in range(n):
                        s = dot(key_block(kv_ref, 0, j), q, NT)
                        prob = jnp.exp2(s * SCALE2 - norm)
                        if j == 0:
                            prob = jnp.where(allowed, prob, 0.0)
                        dprob = dot(key_block(kv_ref, 1, j), cot, NT)
                        prob_ref[other, x, j] = prob.astype(BF)
                        score_ref[other, x, j] = (prob * (dprob - delta)).astype(BF)
                    blocks(score_ref, score_hbm, n, other, x, sems).start()
            return 0

        lax.fori_loop(0, 2, sources, 0)
        for s in range(SLOTS):
            for kind, left_ref, scale in ((0, score_ref, 1.0), (1, prob_ref, 1.0 / SCALE)):
                if s < n:
                    total = (over_sources(left_ref, kind * COLS, s) * scale).astype(BF)
                else:
                    total = jnp.zeros((KEYS, HEAD), BF)
                for r in range(GROUP):
                    dkv_ref[2 * r + kind, s * HALF : (s + 1) * HALF, :] = total[
                        r * HALF : (r + 1) * HALF
                    ]
        for other in range(2):
            for x in range(4):
                blocks(score_ref, score_hbm, n, other, x, sems).wait()

    by_count(place, body)


def query_gradients(
    kv_ref, score_hbm, same_ref, other_ref, turned_ref, score_ref, sems
):

    def body(n):
        for x in range(4):
            for other in (1, 0):
                blocks(score_hbm, score_ref, n, other, x, sems).start()
        for s in range(n):
            turned_ref[s] = key_block(kv_ref, 0, s).astype(F32).T.astype(BF)

        def sources(x, _):
            for other, dq_ref in ((1, other_ref), (0, same_ref)):
                blocks(score_hbm, score_ref, n, other, x, sems).wait()
                dq = dot(turned_ref[0], score_ref[other, x, 0], NN)
                for j in range(1, n):
                    dq += dot(turned_ref[j], score_ref[other, x, j], NN)
                dq_ref[x] = dq.astype(BF)
            return 0

        lax.fori_loop(0, 4, sources, 0)

    by_count(position(), body)


def sum_keys(dkv_ref, own_ref, one_ref, two_ref):
    for s, ref in enumerate((own_ref, one_ref, two_ref)):
        for half in range(2):
            total = dkv_ref[half, s * HALF : (s + 1) * HALF, :].astype(F32)
            for r in range(1, GROUP):
                total += dkv_ref[2 * r + half, s * HALF : (s + 1) * HALF, :].astype(F32)
            ref[half * HALF : (half + 1) * HALF, :] = total.astype(ref.dtype)


def sum_cores(same_ref, other_ref, out_ref):
    out_ref[...] = (same_ref[...].astype(F32) + other_ref[...].astype(F32)).astype(BF)


def finish_keys(own_ref, two_ref, one_ref, out_ref):
    out_ref[...] = (
        own_ref[...] + one_ref[...].astype(F32) + two_ref[...].astype(F32)
    ).astype(BF)


def finish_queries(dq_ref, out_ref):
    total = dq_ref[0].astype(F32)
    for x in range(1, 4):
        total += dq_ref[x].astype(F32)
    for h in range(HEADS):
        lanes = slice(h * HEAD, (h + 1) * HEAD)
        out_ref[:, lanes] = total[:, lanes].T.astype(BF)


def local_kernels(same, other, kv, exchange):
    segs = [pltpu.VMEM((TOK, TOK), F32), pltpu.VMEM((KEYS, TOK), F32)]
    norms = call(
        row_sums, "row_sums", pltpu.VMEM((8, 2, 4, HEADS, TOK), F32), segs, near=range(3)
    )(same, other, kv)
    norms = exchange(norms)
    dkv, scores = call(
        key_gradients,
        "key_gradients",
        (pltpu.VMEM((2 * GROUP, SLOTS * HALF, HEAD), BF), pltpu.HBM(FULL, BF)),
        segs
        + [
            pltpu.VMEM((2, 4, HEADS, TOK), F32),
            pltpu.VMEM(FULL, BF),
            pltpu.VMEM(FULL, BF),
            pltpu.SemaphoreType.DMA((2, 4)),
        ],
        near=range(4),
        far_out=(1,),
    )(same, other, kv, norms)
    dq_same, dq_other = call(
        query_gradients,
        "query_gradients",
        (pltpu.VMEM((4, HEAD, COLS), BF), pltpu.VMEM((4, HEAD, COLS), BF)),
        [
            pltpu.VMEM((SLOTS, HEAD, KEYS), BF),
            pltpu.VMEM(FULL, BF),
            pltpu.SemaphoreType.DMA((2, 4)),
        ],
        near=(0,),
        far=(1,),
    )(kv, scores)
    return dkv, dq_same, dq_other


def per_device(queries, stored_key_value, out_grad, attn_out, segment_ids, loss_mask):
    seg = segment_ids.reshape(1, TOK)
    mask = loss_mask.reshape(1, TOK)
    swap = [(0, 1), (1, 0)]

    two = lax.ppermute(stored_key_value, Z_AXES, FAR)
    one = lax.ppermute(stored_key_value, "zg", [(0, 1), (1, 2)])
    wide = pltpu.VMEM((TOK, HEADS * HEAD), BF)
    line = pltpu.VMEM((1, TOK), jnp.int32)
    packed, own = call(
        pack_queries,
        "pack_queries",
        (pltpu.VMEM((Q_ROWS, HEAD), BF), pltpu.VMEM((TOK + 16, HEAD), BF)),
        [wide, wide, wide, line, line, pltpu.VMEM((TOK, HEAD), BF), pltpu.SemaphoreType.DMA((6,))],
        far=range(6),
    )(queries, out_grad, attn_out, seg, mask, stored_key_value)
    near = lax.ppermute(packed, "pair", swap)
    across = [(i, 3 - i) for i in range(4)]
    both = lax.ppermute(packed, X_AXES, across)
    far = lax.ppermute(near, X_AXES, across)
    same = call(
        gather_sources, "gather_sources", pltpu.VMEM((4, Q_ROWS, HEAD), BF), near=range(4), cost=LONG
    )(both, far, near, packed)
    other = lax.ppermute(same, "core", swap)
    kv = call(
        pack_keys, "pack_keys", pltpu.VMEM((2 * GROUP, KV_ROWS, HEAD), BF), near=range(3), cost=LONG
    )(
        own, one, two
    )
    kv = lax.all_to_all(kv, ("zr", "pair"), 0, 0, tiled=True).reshape(GROUP, 2, KV_ROWS, HEAD)

    dkv, dq_same, dq_other = local_kernels(
        same, other, kv, lambda norms: lax.all_to_all(norms, PLANE, 0, 0, tiled=True)
    )
    dkv = lax.all_to_all(dkv, ("zr", "pair"), 0, 0, tiled=True)
    dq_other = lax.ppermute(dq_other, "core", swap)
    dq = call(sum_cores, "sum_cores", pltpu.VMEM((4, HEAD, COLS), BF), near=(0, 1))(
        dq_same, dq_other
    )
    dkv, dq = lax.optimization_barrier((dkv, dq))
    own, one, two = call(
        sum_keys,
        "sum_keys",
        (
            pltpu.VMEM((TOK, HEAD), F32),
            pltpu.VMEM((TOK, HEAD), BF),
            pltpu.VMEM((TOK, HEAD), BF),
        ),
        near=(0,),
    )(dkv)
    two = lax.ppermute(two, Z_AXES, [(b, a) for a, b in FAR])
    one = lax.ppermute(one, "zg", [(1, 0), (2, 1)])
    dq = lax.all_to_all(dq, X_AXES, 0, 0, tiled=True)
    kv_grad = call(
        finish_keys, "finish_keys", shape((TOK, HEAD), BF), near=range(3), cost=LONG
    )(own, two, one)
    dq, kv_grad = lax.optimization_barrier((dq, kv_grad))
    query_gradient = call(
        finish_queries, "finish_queries", shape((TOK, HEADS * HEAD), BF), near=(0,)
    )(dq)
    return query_gradient, kv_grad


def solution(mesh):
    fine = Mesh(
        mesh.devices.reshape(4, 4, 2, 2, 4, 2), ("zg", "zr", "xh", "core", "tp", "pair")
    )
    rows = ("zg", "zr", "xh", "core")
    wide = P(rows, ("tp", "pair"))
    return jax.shard_map(
        per_device,
        mesh=fine,
        in_specs=(wide, wide, wide, wide, P(rows), P(rows)),
        out_specs=(wide, wide),
        check_vma=False,
    )
```

```python
import functools
import math

import jax
import jax.numpy as jnp
from jax import lax
from jax.experimental import pallas as pl
from jax.experimental.pallas import tpu as pltpu
from jax.sharding import Mesh, PartitionSpec as P

BF = jnp.bfloat16
F32 = jnp.float32
NEGATIVE = -1e30
TOK = 128
HEAD = 128
HEADS = 4
COLS = HEADS * TOK
GROUP = 4
SLOTS = 3
HALF = TOK // 2
KEYS = GROUP * HALF
Q_ROWS = 2 * COLS + 16
KV_ROWS = SLOTS * HALF
FULL = (2, 4, SLOTS, KEYS, COLS)
SCALE = 1.0 / math.sqrt(HEAD)
SCALE2 = SCALE * math.log2(math.e)
LOG_SCALE = math.log2(SCALE)
X_AXES = ("xh", "pair")
Z_AXES = ("zg", "zr")
FAR = [(r, 8 + (r + 2) % 4) for r in range(4)]
PLANE = ("xh", "core", "pair")
NT = (((1,), (1,)), ((), ()))
NN = (((1,), (0,)), ((), ()))
VMEM_LIMIT = 40 * 1024 * 1024
LONG = pl.CostEstimate(flops=40_000_000_000, bytes_accessed=120_000_000, transcendentals=0)


def dot(a, b, dims):
    return lax.dot_general(a, b, dims, preferred_element_type=F32)


def call(kernel, name, out_shape, scratch=(), near=(), far=(), far_out=(), cost=None):
    def bound(*args):
        specs = [
            pl.BlockSpec(memory_space=pltpu.HBM if i in far else pltpu.VMEM)
            for i in range(len(args))
        ]
        outs = out_shape if isinstance(out_shape, tuple) else (out_shape,)
        out_specs = tuple(
            pl.BlockSpec(memory_space=pltpu.HBM if i in far_out else pltpu.VMEM)
            for i in range(len(outs))
        )
        kept = [
            pltpu.with_memory_space_constraint(a, pltpu.VMEM if i in near else pltpu.HBM)
            for i, a in enumerate(args)
        ]
        run = pl.pallas_call(
            kernel,
            out_shape=outs,
            in_specs=specs,
            out_specs=out_specs,
            scratch_shapes=scratch,
            name=name,
            cost_estimate=cost,
            compiler_params=pltpu.CompilerParams(vmem_limit_bytes=VMEM_LIMIT),
        )
        got = run(*kept)
        return got if isinstance(out_shape, tuple) else got[0]

    return bound


def shape(dims, dtype):
    return jax.ShapeDtypeStruct(dims, dtype)


def pack_queries(
    q_hbm, g_hbm, o_hbm, seg_hbm, mask_hbm, kv_hbm,
    out_ref, own_ref,
    q_ref, g_ref, o_ref, seg_ref, mask_ref, kv_ref, sems,
):
    copies = [
        pltpu.make_async_copy(far, ref, sems.at[i])
        for i, (far, ref) in enumerate(
            (
                (q_hbm, q_ref),
                (mask_hbm, mask_ref),
                (seg_hbm, seg_ref),
                (g_hbm, g_ref),
                (o_hbm, o_ref),
                (kv_hbm, kv_ref),
            )
        )
    ]
    for copy in copies:
        copy.start()
    copies[0].wait()
    for h in range(HEADS):
        out_ref[h * TOK : (h + 1) * TOK, :] = q_ref[:, h * HEAD : (h + 1) * HEAD]
    for copy in copies[1:]:
        copy.wait()
    mask = jnp.broadcast_to(mask_ref[...].astype(F32), (TOK, TOK)).T
    rows = []
    for h in range(HEADS):
        lanes = slice(h * HEAD, (h + 1) * HEAD)
        cot = g_ref[:, lanes].astype(F32) * mask
        rows.append(jnp.sum((cot * o_ref[:, lanes].astype(F32)).T, axis=0, keepdims=True))
        out_ref[COLS + h * TOK : COLS + (h + 1) * TOK, :] = cot.astype(BF)
    delta = jnp.concatenate(rows, axis=0)
    high = delta.astype(BF).astype(F32)
    low = delta - high
    seg = seg_ref[...].astype(F32)
    out_ref[2 * COLS :, :] = jnp.concatenate(
        [high, low, seg, jnp.zeros((7, TOK), F32)], axis=0
    ).astype(BF)
    own_ref[:TOK, :] = kv_ref[...]
    own_ref[TOK:, :] = jnp.concatenate([seg, jnp.zeros((15, TOK), F32)], axis=0).astype(BF)


def gather_sources(both_ref, far_ref, near_ref, own_ref, out_ref):
    place = position()
    own = 2 * place[2] + place[4]
    for step, ref in enumerate((own_ref, near_ref, far_ref, both_ref)):
        out_ref[own ^ step] = ref[...]


def pack_keys(own_ref, one_ref, two_ref, out_ref):
    tail = own_ref[TOK:, :]
    for s, ref in enumerate((own_ref, one_ref, two_ref)):
        for half in range(2):
            part = ref[half * HALF : (half + 1) * HALF, :]
            for r in range(GROUP):
                out_ref[2 * r + half, s * HALF : (s + 1) * HALF, :] = part

    @pl.when(lax.axis_index("zg") == 3)
    def _():
        for i in range(2 * GROUP):
            out_ref[i, HALF : HALF + 16, :] = tail


def position():
    return (
        lax.axis_index("zg"),
        lax.axis_index("zr"),
        lax.axis_index("xh"),
        lax.axis_index("core"),
        lax.axis_index("pair"),
    )


def slot_count(zg):
    return jnp.where(zg == 3, 1, zg + 1)


def key_block(kv_ref, kind, s):
    first = s * HALF if isinstance(s, int) else pl.multiple_of(s * HALF, HALF)
    return kv_ref[:, kind, pl.ds(first, HALF), :].reshape(KEYS, HEAD)


def key_segments(kv_ref, pair, turn_ref, seg_ref):
    for r in range(GROUP):
        row = kv_ref[r, 0, HALF : HALF + 16, :].astype(F32)[0:1]
        turn_ref[...] = jnp.broadcast_to(row, (TOK, TOK)).T
        seg_ref[r * HALF : (r + 1) * HALF, :] = turn_ref[
            pl.ds(pl.multiple_of(pair * HALF, HALF), HALF), :
        ]


def allowed_pairs(place, query_seg, hx, from_core, seg_ref):
    zg, zr, xh, core, pair = place
    row = lax.broadcasted_iota(jnp.int32, (KEYS, TOK), 0)
    key_pos = (row // HALF) * 512 + row % HALF + ((2 * xh + core) * TOK + pair * HALF)
    lane = lax.broadcasted_iota(jnp.int32, (KEYS, TOK), 1)
    query_pos = lane + (zr * 512 + (2 * hx + from_core) * TOK)
    one_document = jnp.broadcast_to(zg, (KEYS, TOK)) < 3
    return (key_pos <= query_pos) & ((seg_ref[...] == query_seg) | one_document)


def tiled(mask):
    return jnp.concatenate([mask] * HEADS, axis=1)


def by_count(place, body):
    count = slot_count(place[0])
    for n in (1, 2, 3):

        @pl.when(count == n)
        def _(n=n):
            body(n)


def flat(rows):
    return jnp.concatenate([rows[h : h + 1] for h in range(HEADS)], axis=1)


def blocks(from_ref, to_ref, n, other, x, sems):
    return pltpu.make_async_copy(
        from_ref.at[other, x, pl.ds(0, n)], to_ref.at[other, x, pl.ds(0, n)], sems.at[other, x]
    )


def row_sums(
    same_ref, other_ref, kv_ref, out_ref, turn_ref, seg_ref
):
    place = position()
    core, pair = place[3:]
    key_segments(kv_ref, pair, turn_ref, seg_ref)

    def body(n):
        def sources(hx):
            for other, q_ref in enumerate((same_ref, other_ref)):
                from_core = (1 - core) if other else core
                segs = q_ref[2 * hx, 2 * COLS :, :].astype(F32)[8:9]
                allowed = tiled(allowed_pairs(place, segs, hx, from_core, seg_ref))
                for p in range(2):
                    x = 2 * hx + p
                    q = q_ref[x, :COLS, :]
                    scores = [dot(key_block(kv_ref, 0, j), q, NT) * SCALE2 for j in range(n)]
                    scores[0] = jnp.where(allowed, scores[0], NEGATIVE)
                    top = jnp.full((1, COLS), 0.1 * NEGATIVE, F32)
                    for s in scores:
                        top = jnp.maximum(top, jnp.max(s, axis=0, keepdims=True))
                    total = jnp.zeros((1, COLS), F32)
                    for s in scores:
                        total += jnp.sum(jnp.exp2(s - top), axis=0, keepdims=True)
                    norm = jnp.maximum(top + jnp.log2(total), NEGATIVE)
                    for h in range(HEADS):
                        lanes = slice(h * TOK, (h + 1) * TOK)
                        piece = jnp.broadcast_to(norm[:, lanes], (8, TOK))
                        out_ref[:, from_core, x, h : h + 1, :] = piece.reshape(8, 1, TOK)

        sources(0)
        sources(1)

    by_count(place, body)


def key_gradients(
    same_ref, other_ref, kv_ref, norm_ref,
    dkv_ref, score_hbm,
    turn_ref, seg_ref, log_ref, prob_ref, score_ref, sems,
):
    place = position()
    core, pair = place[3:]
    key_segments(kv_ref, pair, turn_ref, seg_ref)
    norms = norm_ref[...]
    top = jnp.max(norms, axis=0)
    log_ref[...] = top + jnp.log2(jnp.sum(jnp.exp2(norms - top[None]), axis=0)) - LOG_SCALE

    def over_sources(left_ref, first, j):
        total = None
        for other, right_ref in enumerate((same_ref, other_ref)):
            for x in range(4):
                part = dot(left_ref[other, x, j], right_ref[x, first : first + COLS, :], NN)
                total = part if total is None else total + part
        return total

    def body(n):
        def sources(hx):
            for other, q_ref in enumerate((same_ref, other_ref)):
                from_core = (1 - core) if other else core
                segs = q_ref[2 * hx, 2 * COLS :, :].astype(F32)[8:9]
                allowed = tiled(allowed_pairs(place, segs, hx, from_core, seg_ref))
                for p in range(2):
                    x = 2 * hx + p
                    q = q_ref[x, :COLS, :]
                    cot = q_ref[x, COLS : 2 * COLS, :]
                    tail = q_ref[x, 2 * COLS :, :].astype(F32)
                    delta = flat(tail[0:HEADS] + tail[HEADS : 2 * HEADS])
                    norm = flat(log_ref[from_core, x])
                    for j in range(n):
                        s = dot(key_block(kv_ref, 0, j), q, NT)
                        prob = jnp.exp2(s * SCALE2 - norm)
                        if j == 0:
                            prob = jnp.where(allowed, prob, 0.0)
                        dprob = dot(key_block(kv_ref, 1, j), cot, NT)
                        prob_ref[other, x, j] = prob.astype(BF)
                        score_ref[other, x, j] = (prob * (dprob - delta)).astype(BF)
                    blocks(score_ref, score_hbm, n, other, x, sems).start()

        sources(0)
        sources(1)
        for s in range(SLOTS):
            for kind, left_ref, scale in ((0, score_ref, 1.0), (1, prob_ref, 1.0 / SCALE)):
                if s < n:
                    total = (over_sources(left_ref, kind * COLS, s) * scale).astype(BF)
                else:
                    total = jnp.zeros((KEYS, HEAD), BF)
                for r in range(GROUP):
                    dkv_ref[2 * r + kind, s * HALF : (s + 1) * HALF, :] = total[
                        r * HALF : (r + 1) * HALF
                    ]
        for other in range(2):
            for x in range(4):
                blocks(score_ref, score_hbm, n, other, x, sems).wait()

    by_count(place, body)


def query_gradients(
    kv_ref, score_hbm, same_ref, other_ref, turned_ref, score_ref, sems
):

    def body(n):
        for x in range(4):
            for other in (1, 0):
                blocks(score_hbm, score_ref, n, other, x, sems).start()
        for s in range(n):
            turned_ref[s] = key_block(kv_ref, 0, s).astype(F32).T.astype(BF)

        def sources(x, _):
            for other, dq_ref in ((1, other_ref), (0, same_ref)):
                blocks(score_hbm, score_ref, n, other, x, sems).wait()
                dq = dot(turned_ref[0], score_ref[other, x, 0], NN)
                for j in range(1, n):
                    dq += dot(turned_ref[j], score_ref[other, x, j], NN)
                dq_ref[x] = dq.astype(BF)
            return 0

        lax.fori_loop(0, 4, sources, 0)

    by_count(position(), body)


def sum_keys(dkv_ref, own_ref, one_ref, two_ref):
    for s, ref in enumerate((own_ref, one_ref, two_ref)):
        for half in range(2):
            total = dkv_ref[half, s * HALF : (s + 1) * HALF, :].astype(F32)
            for r in range(1, GROUP):
                total += dkv_ref[2 * r + half, s * HALF : (s + 1) * HALF, :].astype(F32)
            ref[half * HALF : (half + 1) * HALF, :] = total.astype(ref.dtype)


def sum_cores(same_ref, other_ref, out_ref):
    out_ref[...] = (same_ref[...].astype(F32) + other_ref[...].astype(F32)).astype(BF)


def finish_keys(own_ref, two_ref, one_ref, out_ref):
    out_ref[...] = (
        own_ref[...] + one_ref[...].astype(F32) + two_ref[...].astype(F32)
    ).astype(BF)


def finish_queries(dq_ref, out_ref):
    total = dq_ref[0].astype(F32)
    for x in range(1, 4):
        total += dq_ref[x].astype(F32)
    for h in range(HEADS):
        lanes = slice(h * HEAD, (h + 1) * HEAD)
        out_ref[:, lanes] = total[:, lanes].T.astype(BF)


def local_kernels(same, other, kv, exchange):
    segs = [pltpu.VMEM((TOK, TOK), F32), pltpu.VMEM((KEYS, TOK), F32)]
    norms = call(
        row_sums, "row_sums", pltpu.VMEM((8, 2, 4, HEADS, TOK), F32), segs, near=range(3)
    )(same, other, kv)
    norms = exchange(norms)
    dkv, scores = call(
        key_gradients,
        "key_gradients",
        (pltpu.VMEM((2 * GROUP, SLOTS * HALF, HEAD), BF), pltpu.HBM(FULL, BF)),
        segs
        + [
            pltpu.VMEM((2, 4, HEADS, TOK), F32),
            pltpu.VMEM(FULL, BF),
            pltpu.VMEM(FULL, BF),
            pltpu.SemaphoreType.DMA((2, 4)),
        ],
        near=range(4),
        far_out=(1,),
    )(same, other, kv, norms)
    dq_same, dq_other = call(
        query_gradients,
        "query_gradients",
        (pltpu.VMEM((4, HEAD, COLS), BF), pltpu.VMEM((4, HEAD, COLS), BF)),
        [
            pltpu.VMEM((SLOTS, HEAD, KEYS), BF),
            pltpu.VMEM(FULL, BF),
            pltpu.SemaphoreType.DMA((2, 4)),
        ],
        near=(0,),
        far=(1,),
    )(kv, scores)
    return dkv, dq_same, dq_other


def per_device(queries, stored_key_value, out_grad, attn_out, segment_ids, loss_mask):
    seg = segment_ids.reshape(1, TOK)
    mask = loss_mask.reshape(1, TOK)
    swap = [(0, 1), (1, 0)]

    two = lax.ppermute(stored_key_value, Z_AXES, FAR)
    one = lax.ppermute(stored_key_value, "zg", [(0, 1), (1, 2)])
    wide = pltpu.VMEM((TOK, HEADS * HEAD), BF)
    line = pltpu.VMEM((1, TOK), jnp.int32)
    packed, own = call(
        pack_queries,
        "pack_queries",
        (pltpu.VMEM((Q_ROWS, HEAD), BF), pltpu.VMEM((TOK + 16, HEAD), BF)),
        [wide, wide, wide, line, line, pltpu.VMEM((TOK, HEAD), BF), pltpu.SemaphoreType.DMA((6,))],
        far=range(6),
    )(queries, out_grad, attn_out, seg, mask, stored_key_value)
    near = lax.ppermute(packed, "pair", swap)
    across = [(i, 3 - i) for i in range(4)]
    both = lax.ppermute(packed, X_AXES, across)
    far = lax.ppermute(near, X_AXES, across)
    same = call(
        gather_sources, "gather_sources", pltpu.VMEM((4, Q_ROWS, HEAD), BF), near=range(4), cost=LONG
    )(both, far, near, packed)
    other = lax.ppermute(same, "core", swap)
    kv = call(
        pack_keys, "pack_keys", pltpu.VMEM((2 * GROUP, KV_ROWS, HEAD), BF), near=range(3), cost=LONG
    )(
        own, one, two
    )
    kv = lax.all_to_all(kv, ("zr", "pair"), 0, 0, tiled=True).reshape(GROUP, 2, KV_ROWS, HEAD)

    dkv, dq_same, dq_other = local_kernels(
        same, other, kv, lambda norms: lax.all_to_all(norms, PLANE, 0, 0, tiled=True)
    )
    dkv = lax.all_to_all(dkv, ("zr", "pair"), 0, 0, tiled=True)
    dq_other = lax.ppermute(dq_other, "core", swap)
    dq = call(sum_cores, "sum_cores", pltpu.VMEM((4, HEAD, COLS), BF), near=(0, 1))(
        dq_same, dq_other
    )
    dkv, dq = lax.optimization_barrier((dkv, dq))
    own, one, two = call(
        sum_keys,
        "sum_keys",
        (
            pltpu.VMEM((TOK, HEAD), F32),
            pltpu.VMEM((TOK, HEAD), BF),
            pltpu.VMEM((TOK, HEAD), BF),
        ),
        near=(0,),
    )(dkv)
    two = lax.ppermute(two, Z_AXES, [(b, a) for a, b in FAR])
    one = lax.ppermute(one, "zg", [(1, 0), (2, 1)])
    dq = lax.all_to_all(dq, X_AXES, 0, 0, tiled=True)
    kv_grad = call(
        finish_keys, "finish_keys", shape((TOK, HEAD), BF), near=range(3), cost=LONG
    )(own, two, one)
    dq, kv_grad = lax.optimization_barrier((dq, kv_grad))
    query_gradient = call(
        finish_queries, "finish_queries", shape((TOK, HEADS * HEAD), BF), near=(0,)
    )(dq)
    return query_gradient, kv_grad


def solution(mesh):
    fine = Mesh(
        mesh.devices.reshape(4, 4, 2, 2, 4, 2), ("zg", "zr", "xh", "core", "tp", "pair")
    )
    rows = ("zg", "zr", "xh", "core")
    wide = P(rows, ("tp", "pair"))
    return jax.shard_map(
        per_device,
        mesh=fine,
        in_specs=(wide, wide, wide, wide, P(rows), P(rows)),
        out_specs=(wide, wide),
        check_vma=False,
    )
```
